512 devices in a mesh: tm: 8 (over y, z_hi), space: 64 (over x, z_lo, core).
Axes of the slice: x: 4, y: 4, z: 16 (z_hi: 2, z_lo: 8; z = z_hi * 8 + z_lo), core: 2. Of those that a mesh axis runs over, the one named last changes fastest.
Arguments:
- start_state: float32 [8, 3, 512, 2048], P('tm', None, 'space'), may hold values from -4 to 4
- vertical_field: float32 [512, 2048], P('space'), may hold values from -1 to 1
Outputs:
- new_start: float32 [8, 3, 512, 2048], P('tm', None, 'space')
- fine_end: float32 [8, 3, 512, 2048], P('tm', None, 'space')
- coarse_end: float32 [8, 3, 512, 2048], P('tm', None, 'space')
The draws below stay inside these ranges and needn't reach their ends.
All inputs are finite; a program needn't handle non-finite values.
Results may differ from the reference program's by a relative error of at most 0.0001.
Values sent between devices are 32-bit elements; how exact they have to be, the bound alone decides.
No kernel may reach another device: no remote copies, remote signals or barrier semaphores. Data moves between devices by JAX's collectives and lax.ppermute only.
A program may use at most 64 MiB of HBM per device.

```python
import jax
import jax.numpy as jnp
from jax import lax

COLS = 2048
FINE_STEPS = 8
GRID_ROWS = 512
SLICES = 8


def levels(own_key, shape, pieces, low, largest):
    gain = 1.0
    for dim, blocks in pieces:
        draws = jax.random.uniform(jax.random.fold_in(jax.random.fold_in(own_key, 6), dim), (blocks,), jnp.float32, low / len(pieces), largest / len(pieces))
        gain = gain * jnp.repeat(jnp.exp(draws), shape[dim] // blocks).reshape((-1,) + (1,) * (len(shape) - 1 - dim))
    return gain


def noise(stream_key, shape, scale, reach, cuts=(), kind=jnp.bfloat16):
    result = scale * jax.random.normal(stream_key, shape, jnp.float32)
    if cuts:
        result = result * levels(stream_key, shape, cuts, -0.22, 0.18)
    return jnp.clip(result, -reach, reach).astype(kind)


def setup_inputs(seed: int = 0) -> dict:
    arg_keys = jax.random.split(jax.random.key(seed), 3)
    return {
        "start_state": noise(arg_keys[0], (SLICES, 3, GRID_ROWS, COLS), 1.0, 4.0, ((0, 8), (2, 64)), jnp.float32),
        "vertical_field": jnp.clip(jax.random.uniform(arg_keys[1], (GRID_ROWS, COLS), jnp.float32, -1.0, 1.0) * levels(arg_keys[1], (GRID_ROWS, COLS), ((0, 64),), -0.4, 0.0), -1.0, 1.0),
    }


lorentz = 0.3
friction = 0.01
time_step = 0.28


def mirror(fields):
    row_signs = jnp.array([1.0, -1.0, 1.0], fields.dtype)[:, None, None]
    col_signs = jnp.array([1.0, 1.0, -1.0], fields.dtype)[:, None, None]
    fields = jnp.concatenate([fields[:, :1] * row_signs, fields, fields[:, -1:] * row_signs], axis=1)
    return jnp.concatenate([fields[:, :, :1] * col_signs, fields, fields[:, :, -1:] * col_signs], axis=2)


def tendency(padded, magnetic, factor):
    height = padded[0]
    flow_east = padded[1]
    flow_north = padded[2]

    def along_rows(values):
        return (values[2:, 1:-1] - values[:-2, 1:-1]) * factor

    def along_cols(values):
        return (values[1:-1, 2:] - values[1:-1, :-2]) * factor

    slope_east = along_rows(height)
    slope_north = along_cols(height)
    rise_rate = -(along_rows(flow_east) + along_cols(flow_north))
    push_east = -slope_east + lorentz * magnetic * slope_north - friction * flow_east[1:-1, 1:-1]
    push_north = -slope_north - lorentz * magnetic * slope_east - friction * flow_north[1:-1, 1:-1]
    return jnp.stack([rise_rate, push_east, push_north])


def runge_kutta(fields, rates_of, length):
    first_segment = fields + length * rates_of(fields)
    second_segment = 0.75 * fields + 0.25 * (first_segment + length * rates_of(first_segment))
    return fields / 3.0 + (2.0 / 3.0) * (second_segment + length * rates_of(second_segment))


def restrict_state(fields):
    shape_in = fields.shape
    return fields.reshape(shape_in[0], shape_in[1] // 2, 2, shape_in[2] // 2, 2).mean(axis=(2, 4))


def restrict_field(magnetic):
    shape_in = magnetic.shape
    return magnetic.reshape(shape_in[0] // 2, 2, shape_in[1] // 2, 2).mean(axis=(1, 3))


def prolong(coarse_fields):
    shape_in = coarse_fields.shape
    expanded = jnp.broadcast_to(coarse_fields[:, :, None, :, None], (shape_in[0], shape_in[1], 2, shape_in[2], 2))
    return expanded.reshape(shape_in[0], 2 * shape_in[1], 2 * shape_in[2])


def fine_run(anchor, magnetic):
    def advance(counter, fields):
        return runge_kutta(fields, lambda values: tendency(mirror(values), magnetic, 0.5), time_step)

    return lax.fori_loop(0, FINE_STEPS, advance, anchor)


def coarse_run(fields, coarse_field):
    coarse_fields = runge_kutta(restrict_state(fields), lambda values: tendency(mirror(values), coarse_field, 0.25), FINE_STEPS * time_step)
    return prolong(coarse_fields)


def reference(start_state, vertical_field):
    coarse_field = restrict_field(vertical_field)
    fine_end = lax.map(lambda anchor: fine_run(anchor, vertical_field), start_state)
    coarse_end = lax.map(lambda anchor: coarse_run(anchor, coarse_field), start_state)
    defect = fine_end - coarse_end

    def link(current, correction):
        advanced = coarse_run(current, coarse_field) + correction
        return advanced, advanced

    final_fields, following = lax.scan(link, start_state[0], defect[:-1])
    new_start = jnp.concatenate([start_state[:1], following], axis=0)
    return new_start, fine_end, coarse_end
```

```python
import functools

import jax
import jax.numpy as jnp
from jax import lax
from jax.experimental import pallas as pl
from jax.experimental.pallas import tpu as pltpu
from jax.sharding import PartitionSpec as P

FINE_STEPS = 8
LORENTZ = 0.3
FRICTION = 0.01
TIME_STEP = 0.28
ROWS = 8
LANES = 128

ALPHA = 0.6265382932707997
QUAD_A = 0.3734617067292003
QUAD_B = 0.2660119396638869

VMEM = pl.BlockSpec(memory_space=pltpu.VMEM)
SMEM = pl.BlockSpec(memory_space=pltpu.SMEM)


def iotas():
    sub = lax.broadcasted_iota(jnp.int32, (ROWS, LANES), 0)
    lane = lax.broadcasted_iota(jnp.int32, (ROWS, LANES), 1)
    return sub, lane


def strip(k):
    start = LANES + k * LANES
    return pl.ds(start if isinstance(start, int) else pl.multiple_of(start, LANES), LANES)


def guards(buf, tiles, shift, strips):
    for t in tiles:
        for comp, sign in ((0, 1.0), (2, -1.0)):
            first = buf[t, comp, :, strip(0)]
            last = buf[t, comp, :, strip(strips - 1)]
            buf[t, comp, :, strip(-1)] = sign * pltpu.roll(first, LANES - shift, 1)
            buf[t, comp, :, strip(strips)] = sign * pltpu.roll(last, shift, 1)


def stage(dst, src, base, weight, length, field, tiles, shift, cell, strips, group):
    factor = length / (2.0 * cell)
    drag = FRICTION * length
    sub, lane = iotas()
    rows_high = sub >= ROWS - shift
    rows_low = sub < shift
    lanes_high = lane >= LANES - shift
    lanes_low = lane < shift
    slots = dst.shape[0]

    def block(g, carry):
        for j in range(group):
            k = g * group + j
            here = strip(k)
            cache = {}

            def get(comp, t):
                t = min(max(t, 0), slots - 1)
                if (comp, t) not in cache:
                    cache[comp, t] = src[t, comp, :, here]
                return cache[comp, t]

            for t in tiles:
                height, east, north = get(0, t), get(1, t), get(2, t)

                def row_diff(comp, centre):
                    before = jnp.where(rows_high, get(comp, t - 1), centre)
                    after = jnp.where(rows_low, get(comp, t + 1), centre)
                    return pltpu.roll(after, ROWS - shift, 0) - pltpu.roll(before, shift, 0)

                def col_diff(comp, centre):
                    before = jnp.where(lanes_high, src[t, comp, :, strip(k - 1)], centre)
                    after = jnp.where(lanes_low, src[t, comp, :, strip(k + 1)], centre)
                    return pltpu.roll(after, LANES - shift, 1) - pltpu.roll(before, shift, 1)

                b = field[t, :, pl.ds(here.start - LANES, LANES)]
                dx, dy = row_diff(0, height), col_diff(0, height)
                rise = row_diff(1, east) + col_diff(2, north)
                if base is src:
                    new_height = weight * height - factor * rise
                    new_east = (weight - drag) * east + factor * (b * dy - dx)
                    new_north = (weight - drag) * north - factor * (b * dx + dy)
                else:
                    old = [base[t, comp, :, here] for comp in range(3)]
                    if weight != 1.0:
                        old = [weight * o for o in old]
                    new_height = old[0] - factor * rise
                    new_east = old[1] - drag * east + factor * (b * dy - dx)
                    new_north = old[2] - drag * north - factor * (b * dx + dy)
                dst[t, 0, :, here] = new_height
                dst[t, 1, :, here] = new_east
                dst[t, 2, :, here] = new_north
        return carry

    lax.fori_loop(0, strips // group, block, 0)
    guards(dst, tiles, shift, strips)


def pair_mean(x, sub, lane):
    x = x + jnp.where(sub % 2 == 0, pltpu.roll(x, ROWS - 1, 0), pltpu.roll(x, 1, 0))
    x = x + jnp.where(lane % 2 == 0, pltpu.roll(x, LANES - 1, 1), pltpu.roll(x, 1, 1))
    return 0.25 * x


def pack(height, east, north, sub, lane):
    return jnp.where(sub % 2 == 0, jnp.where(lane % 2 == 0, height, east), north)


def unpack(x, sub, lane):
    even = jnp.where(sub % 2 == 0, x, pltpu.roll(x, 1, 0))
    north = jnp.where(sub % 2 == 1, x, pltpu.roll(x, ROWS - 1, 0))
    height = jnp.where(lane % 2 == 0, even, pltpu.roll(even, 1, 1))
    east = jnp.where(lane % 2 == 1, even, pltpu.roll(even, LANES - 1, 1))
    return height, east, north


def flip_tiles(position, count, halo, first, copy_row):
    low = jnp.maximum(halo - position, 0)
    high = jnp.maximum(position + halo - (count - 1), 0)

    def fill_low(q, carry):
        for r in range(ROWS):
            copy_row(first + halo - position - 1 - q, ROWS - 1 - r, first + halo - position + q, r)
        return carry

    def fill_high(q, carry):
        for r in range(ROWS):
            copy_row(
                first + count + q - position + halo,
                ROWS - 1 - r,
                first + count - 1 - q - position + halo,
                r,
            )
        return carry

    lax.fori_loop(0, low, fill_low, 0)
    lax.fori_loop(0, high, fill_high, 0)


def flip_state(buf, position, count, halo, first=0):
    cols = pl.ds(LANES, buf.shape[3] - 2 * LANES)

    def copy_row(t_to, r_to, t_from, r_from):
        for comp, sign in ((0, 1.0), (1, -1.0), (2, 1.0)):
            buf[t_to, comp, pl.ds(r_to, 1), cols] = sign * buf[t_from, comp, pl.ds(r_from, 1), cols]

    flip_tiles(position, count, halo, first, copy_row)


def flip_field(field, position, count, halo):
    def copy_row(t_to, r_to, t_from, r_from):
        field[t_to, pl.ds(r_to, 1), :] = -field[t_from, pl.ds(r_from, 1), :]

    flip_tiles(position, count, halo, 0, copy_row)


def load_window(buf, state, low, high, position, count, strips, shift):
    cols = pl.ds(LANES, strips * LANES)
    for t, ref in ((0, low), (1, state), (2, high)):
        for comp in range(3):
            buf[t, comp, :, cols] = ref[comp]
    flip_state(buf, position, count, 1)
    guards(buf, range(3), shift, strips)


def fine_stages(one, two, field, quads, lines, strips):
    run = functools.partial(stage, field=field, shift=1, cell=1.0, strips=strips, group=4)

    def quad(step, carry):
        run(two, one, one, QUAD_A, QUAD_B * TIME_STEP, tiles=range(3))
        run(one, two, one, 1.0, TIME_STEP, tiles=range(3))
        return carry

    lax.fori_loop(0, quads, quad, 0)
    for n in range(lines):
        tiles = range(3) if n < lines - 1 else (1,)
        run(two, one, one, 1.0, ALPHA * TIME_STEP, tiles=tiles)
        one, two = two, one
    return one


def first_kernel(count, strips, quads, lines, pos, state, field, low, high, out, window, up, down, one, two):
    position = pos[0]
    load_window(one, state, low, high, position, count, strips, 1)
    window[0] = LORENTZ * low[3]
    window[1] = LORENTZ * field[...]
    window[2] = LORENTZ * high[3]
    flip_field(window, position, count, 1)
    up[3] = low[3]
    down[3] = high[3]
    last = fine_stages(one, two, window, quads, lines, strips)
    cols = pl.ds(LANES, strips * LANES)
    for comp in range(3):
        value = last[1, comp, :, cols]
        out[comp] = value
        up[comp] = value
        down[comp] = value


def middle_kernel(count, strips, quads, lines, pos, state, window, low, high, out, up, down, one, two):
    load_window(one, state, low, high, pos[0], count, strips, 1)
    up[3] = low[3]
    down[3] = high[3]
    last = fine_stages(one, two, window, quads, lines, strips)
    cols = pl.ds(LANES, strips * LANES)
    for comp in range(3):
        value = last[1, comp, :, cols]
        out[comp] = value
        up[comp] = value
        down[comp] = value


def last_kernel(
    count, strips, quads, lines, pos, state, window, low, high, coarse, out, detail, packed, one, two
):
    load_window(one, state, low, high, pos[0], count, strips, 1)
    last = fine_stages(one, two, window, quads, lines, strips)
    sub, lane = iotas()
    keep = jnp.where(pos[1] == 0, 0.0, 1.0)
    for k in range(strips):
        lanes = pl.ds(k * LANES, LANES)
        means = []
        for comp in range(3):
            value = last[1, comp, :, strip(k)]
            out[comp, :, lanes] = value
            rest = value - keep * coarse[comp, :, lanes]
            detail[comp, :, lanes] = rest
            means.append(pair_mean(rest, sub, lane))
        packed[:, lanes] = pack(*means, sub, lane)


def coarse_step(bufs, field, tiles_of, strips, group):
    one, two, three = bufs
    length = FINE_STEPS * TIME_STEP
    run = functools.partial(stage, base=one, field=field, shift=2, cell=2.0, strips=strips, group=group)
    run(two, one, weight=1.0, length=length / 3.0, tiles=tiles_of(0))
    run(three, two, weight=1.0, length=length / 2.0, tiles=tiles_of(1))
    run(one, three, weight=1.0, length=length, tiles=tiles_of(2))


def coarse_kernel(count, strips, pos, state, window, low, high, out, one, two, three, mean_field):
    cols = pl.ds(LANES, strips * LANES)
    sub, lane = iotas()
    for t, ref in ((0, low), (1, state), (2, high)):
        for k in range(strips):
            lanes = pl.ds(k * LANES, LANES)
            for comp in range(3):
                one[t, comp, :, strip(k)] = pair_mean(ref[comp, :, lanes], sub, lane)
            mean_field[t, :, lanes] = pair_mean(window[t, :, lanes], sub, lane)
    flip_state(one, pos[0], count, 1)
    guards(one, range(3), 2, strips)
    coarse_step(
        (one, two, three), mean_field, lambda n: range(3) if n < 2 else (1,), strips, 4
    )
    for comp in range(3):
        out[comp] = one[1, comp, :, cols]


def field_kernel(count, strips, pos, window, low2, high2, low3, high3, out):
    sub, lane = iotas()
    for k in range(strips):
        lanes = pl.ds(k * LANES, LANES)
        for t, ref in ((0, low3), (1, low2), (5, high2), (6, high3)):
            out[t, :, lanes] = LORENTZ * pair_mean(ref[3, :, lanes], sub, lane)
        for t in range(3):
            out[t + 2, :, lanes] = pair_mean(window[t, :, lanes], sub, lane)
    flip_field(out, pos[0], count, 3)


def chain_kernel(count, strips, halo, steps, last, pos, field, own, *refs):
    tiles = refs[: 2 * halo + 1]
    refs = refs[2 * halo + 1 :]
    if last:
        detail, packed, anchor, out, one, two, three = refs
    else:
        out, one, two, three = refs
    sub, lane = iotas()
    for t, ref in enumerate(tiles):
        for k in range(strips):
            for comp, value in enumerate(unpack(ref[:, pl.ds(k * LANES, LANES)], sub, lane)):
                one[t, comp, :, strip(k)] = value
    flip_state(one, pos[0], count, halo)
    guards(one, range(2 * halo + 1), 2, strips)
    around = field.at[pl.ds(3 - halo, 2 * halo + 1)]
    for s in range(steps):

        def tiles_of(n, s=s):
            stages_left = 3 * steps - 3 * s - n - 1
            reach = -(-2 * stages_left // ROWS)
            return range(halo - reach, halo + reach + 1)

        coarse_step((one, two, three), around, tiles_of, strips, 2)
    first = pos[1] == 0
    for k in range(strips):
        lanes = pl.ds(k * LANES, LANES)
        values = [one[halo, comp, :, strip(k)] for comp in range(3)]
        extra = unpack(own[:, lanes], sub, lane)
        values = [v + e for v, e in zip(values, extra)]
        if last:
            less = unpack(packed[:, lanes], sub, lane)
            for comp in range(3):
                value = (values[comp] - less[comp]) + detail[comp, :, lanes]
                out[comp, :, lanes] = jnp.where(first, anchor[comp, :, lanes], value)
        else:
            out[:, lanes] = pack(*values, sub, lane)


def call(kernel, outs, buffers, name, *args):
    return pl.pallas_call(
        kernel,
        out_shape=outs,
        in_specs=[SMEM] + [VMEM] * (len(args) - 1),
        out_specs=[VMEM] * len(outs),
        scratch_shapes=buffers,
        compiler_params=pltpu.CompilerParams(vmem_limit_bytes=48 * 1024 * 1024),
        name=name,
    )(*args)


def moved(block, forward, up):
    slices, count = lax.axis_size("tm"), lax.axis_size("space")
    route = [
        ((m * count) + i + up, (m + forward) * count + i)
        for m in range(slices - forward)
        for i in range(count)
        if 0 <= i + up < count
    ]
    return lax.ppermute(block, ("tm", "space"), route)


def body(start_state, vertical_field):
    state = start_state[0]
    cols = state.shape[2]
    strips = cols // LANES
    count = lax.axis_size("space")
    pos = jnp.stack([lax.axis_index("space"), lax.axis_index("tm")]).astype(jnp.int32)
    shape = lambda *dims: jax.ShapeDtypeStruct(dims, jnp.float32)
    tile, message, plane = shape(3, ROWS, cols), shape(4, ROWS, cols), shape(ROWS, cols)
    buf = lambda tiles: pltpu.VMEM((tiles, 3, ROWS, cols + 2 * LANES), jnp.float32)

    sent = jnp.concatenate([state, vertical_field[None]], axis=0)
    low1, high1 = moved(sent, 0, -1), moved(sent, 0, 1)
    mid, window, up, down = call(
        functools.partial(first_kernel, count, strips, 3, 2),
        [tile, shape(3, ROWS, cols), message, message],
        [buf(3), buf(3)],
        "fine_a",
        pos, state, vertical_field, low1, high1,
    )
    low2, high2 = moved(up, 0, -1), moved(down, 0, 1)
    (coarse_end,) = call(
        functools.partial(coarse_kernel, count, strips),
        [tile],
        [buf(3), buf(3), buf(3), pltpu.VMEM((3, ROWS, cols), jnp.float32)],
        "coarse",
        pos, state, window, low1, high1,
    )
    mid, up, down = call(
        functools.partial(middle_kernel, count, strips, 3, 2),
        [tile, message, message],
        [buf(3), buf(3)],
        "fine_b",
        pos, mid, window, low2, high2,
    )
    low3, high3 = moved(up, 0, -1), moved(down, 0, 1)
    fine_end, detail, packed = call(
        functools.partial(last_kernel, count, strips, 2, 4),
        [tile, tile, plane],
        [buf(3), buf(3)],
        "fine_c",
        pos, mid, window, low3, high3, coarse_end,
    )
    around = [0, -1, 1]
    newest = moved(packed, 1, 0)
    older = {j: moved(packed, 2, j) for j in around}
    (coarse_field,) = call(
        functools.partial(field_kernel, count, strips),
        [shape(7, ROWS, cols)],
        [],
        "field",
        pos, window, low2, high2, low3, high3,
    )
    arrived = moved(detail, 1, 0)

    def chain(halo, steps, own, tiles, name):
        order = [tiles[j] for j in range(-halo, halo + 1)]
        return call(
            functools.partial(chain_kernel, count, strips, halo, steps, False),
            [plane],
            [buf(2 * halo + 1)] * 3,
            name,
            pos, coarse_field, own, *order,
        )[0]

    pair = chain(1, 1, newest, older, "chain_a")
    quad = chain(2, 2, pair, {j: moved(pair, 2, j) for j in (0, -1, 1, -2, 2)}, "chain_b")
    far = {j: moved(quad, 4, j) for j in (0, -1, 1, -2, 2, -3, 3)}
    (new_start,) = call(
        functools.partial(chain_kernel, count, strips, 3, 4, True),
        [tile],
        [buf(7)] * 3,
        "chain_c",
        pos, coarse_field, quad, *[far[j] for j in range(-3, 4)], arrived, newest, state,
    )
    return (new_start[None], fine_end[None], coarse_end[None])


def solution(mesh):
    in_specs = (P("tm", None, "space", None), P("space", None))
    out_specs = (
        P("tm", None, "space", None),
        P("tm", None, "space", None),
        P("tm", None, "space", None),
    )
    return jax.shard_map(body, mesh=mesh, in_specs=in_specs, out_specs=out_specs, check_vma=False)
```

```python
import functools

import jax
import jax.numpy as jnp
from jax import lax
from jax.experimental import pallas as pl
from jax.experimental.pallas import tpu as pltpu
from jax.sharding import PartitionSpec as P

FINE_STEPS = 8
LORENTZ = 0.3
FRICTION = 0.01
TIME_STEP = 0.28
ROWS = 8
LANES = 128
GROUP = 8

ALPHA = 0.6265382932707997
QUAD_A = 0.3734617067292003
QUAD_B = 0.2660119396638869

VMEM = pl.BlockSpec(memory_space=pltpu.VMEM)
SMEM = pl.BlockSpec(memory_space=pltpu.SMEM)


def iotas():
    sub = lax.broadcasted_iota(jnp.int32, (ROWS, LANES), 0)
    lane = lax.broadcasted_iota(jnp.int32, (ROWS, LANES), 1)
    return sub, lane


def strip(k):
    start = LANES + k * LANES
    return pl.ds(start if isinstance(start, int) else pl.multiple_of(start, LANES), LANES)


def guards(buf, tiles, shift, strips):
    _, lane = iotas()
    even = lane % 2 == 0
    for t in tiles:
        for comp, sign in ((0, 1.0), (2, -1.0)):
            first = buf[t, comp, :, strip(0)]
            last = buf[t, comp, :, strip(strips - 1)]
            low = sign * pltpu.roll(first, LANES - shift, 1)
            high = sign * pltpu.roll(last, shift, 1)
            if shift == 2:
                low = jnp.where(even, low, pltpu.roll(last, 1, 1))
                high = jnp.where(even, pltpu.roll(first, LANES - 1, 1), high)
            buf[t, comp, :, strip(-1)] = low
            buf[t, comp, :, strip(strips)] = high


def stage(dst, src, base, weight, length, field, tiles, shift, cell, strips, group):
    factor = length / (2.0 * cell)
    drag = FRICTION * length
    sub, lane = iotas()
    rows_high = sub >= ROWS - shift
    rows_low = sub < shift
    lanes_high = lane >= LANES - shift
    lanes_low = lane < shift
    slots = dst.shape[0]
    group = min(group, strips)

    def block(g, carry):
        for j in range(group):
            k = g * group + j
            here = strip(k)
            cache = {}

            def get(comp, t):
                t = min(max(t, 0), slots - 1)
                if (comp, t) not in cache:
                    cache[comp, t] = src[t, comp, :, here]
                return cache[comp, t]

            for t in tiles:
                height, east, north = get(0, t), get(1, t), get(2, t)

                def row_diff(comp, centre):
                    before = jnp.where(rows_high, get(comp, t - 1), centre)
                    after = jnp.where(rows_low, get(comp, t + 1), centre)
                    return pltpu.roll(after, ROWS - shift, 0) - pltpu.roll(before, shift, 0)

                def col_diff(comp, centre):
                    before = jnp.where(lanes_high, src[t, comp, :, strip(k - 1)], centre)
                    after = jnp.where(lanes_low, src[t, comp, :, strip(k + 1)], centre)
                    return pltpu.roll(after, LANES - shift, 1) - pltpu.roll(before, shift, 1)

                b = field[t, :, pl.ds(here.start - LANES, LANES)]
                dx, dy = row_diff(0, height), col_diff(0, height)
                rise = row_diff(1, east) + col_diff(2, north)
                if base is src:
                    new_height = weight * height - factor * rise
                    new_east = (weight - drag) * east + factor * (b * dy - dx)
                    new_north = (weight - drag) * north - factor * (b * dx + dy)
                else:
                    old = [base[t, comp, :, here] for comp in range(3)]
                    if weight != 1.0:
                        old = [weight * o for o in old]
                    new_height = old[0] - factor * rise
                    new_east = old[1] - drag * east + factor * (b * dy - dx)
                    new_north = old[2] - drag * north - factor * (b * dx + dy)
                dst[t, 0, :, here] = new_height
                dst[t, 1, :, here] = new_east
                dst[t, 2, :, here] = new_north
        return carry

    lax.fori_loop(0, strips // group, block, 0)
    guards(dst, tiles, shift, strips)


def pair_mean(x, sub, lane):
    x = x + jnp.where(sub % 2 == 0, pltpu.roll(x, ROWS - 1, 0), pltpu.roll(x, 1, 0))
    x = x + jnp.where(lane % 2 == 0, pltpu.roll(x, LANES - 1, 1), pltpu.roll(x, 1, 1))
    return 0.25 * x


def flip_tiles(position, count, halo, first, copy_row):
    low = jnp.maximum(halo - position, 0)
    high = jnp.maximum(position + halo - (count - 1), 0)

    def fill_low(q, carry):
        for r in range(ROWS):
            copy_row(first + halo - position - 1 - q, ROWS - 1 - r, first + halo - position + q, r)
        return carry

    def fill_high(q, carry):
        for r in range(ROWS):
            copy_row(
                first + count + q - position + halo,
                ROWS - 1 - r,
                first + count - 1 - q - position + halo,
                r,
            )
        return carry

    lax.fori_loop(0, low, fill_low, 0)
    lax.fori_loop(0, high, fill_high, 0)


def flip_state(buf, position, count, halo, first=0):
    cols = pl.ds(LANES, buf.shape[3] - 2 * LANES)

    def copy_row(t_to, r_to, t_from, r_from):
        for comp, sign in ((0, 1.0), (1, -1.0), (2, 1.0)):
            buf[t_to, comp, pl.ds(r_to, 1), cols] = sign * buf[t_from, comp, pl.ds(r_from, 1), cols]

    flip_tiles(position, count, halo, first, copy_row)


def flip_field(field, position, count, halo):
    def copy_row(t_to, r_to, t_from, r_from):
        field[t_to, pl.ds(r_to, 1), :] = -field[t_from, pl.ds(r_from, 1), :]

    flip_tiles(position, count, halo, 0, copy_row)


def folded(left, right, lane):
    return jnp.where(lane % 2 == 0, left, right)


def unfolded(x, lane):
    left = jnp.where(lane % 2 == 0, x, pltpu.roll(x, 1, 1))
    right = jnp.where(lane % 2 == 1, x, pltpu.roll(x, LANES - 1, 1))
    return left, right


def zipped(even, odd, sub):
    return jnp.where(sub % 2 == 0, even, odd)


def unzipped(x, sub):
    even = jnp.where(sub % 2 == 0, x, pltpu.roll(x, 1, 0))
    odd = jnp.where(sub % 2 == 1, x, pltpu.roll(x, ROWS - 1, 0))
    return even, odd


def places(position):
    core = lax.rem(position, 2)
    chip = lax.div(position, 2)
    side = 1 - 2 * core
    near = 2 * (2 * lax.rem(chip, 2) - 1)
    far = 4 * (2 * lax.rem(lax.div(chip, 2), 2) - 1)
    return side, near, far


def fine_kernel(
    count, strips, pos, state, field, near_a, near_b, third, sib, sib_a, sib_b, coarse,
    out, detail, message, one, two, window,
):
    position = pos[0]
    side, near, _ = places(position)
    cols = pl.ds(LANES, strips * LANES)
    arrived = (
        (near_a, near), (near_b, -near), (third, -3 * side),
        (sib, side), (sib_a, near + side), (sib_b, side - near),
    )
    window[3] = LORENTZ * field[...]
    for comp in range(3):
        one[3, comp, :, cols] = state[comp]
    for ref, offset in arrived:
        slot = 3 + offset
        window[slot] = LORENTZ * ref[3]
        for comp in range(3):
            one[slot, comp, :, cols] = ref[comp]
    flip_field(window, position, count, 3)
    flip_state(one, position, count, 3)
    guards(one, range(7), 1, strips)

    run = functools.partial(stage, field=window, shift=1, cell=1.0, strips=strips, group=GROUP)
    a, b = one, two
    for reach, quads, lines in ((3, 3, 2), (2, 3, 2), (1, 2, 4)):
        tiles = range(3 - reach, 4 + reach)

        def quad(step, carry, a=a, b=b, tiles=tiles):
            run(b, a, a, QUAD_A, QUAD_B * TIME_STEP, tiles=tiles)
            run(a, b, a, 1.0, TIME_STEP, tiles=tiles)
            return carry

        lax.fori_loop(0, quads, quad, 0)
        for n in range(lines):
            if n == lines - 1:
                tiles = range(4 - reach, 3 + reach)
            run(b, a, a, 1.0, ALPHA * TIME_STEP, tiles=tiles)
            a, b = b, a

    sub, lane = iotas()
    keep = jnp.where(pos[1] == 0, 0.0, 1.0)
    half = strips // 2
    for k in range(half):
        means = []
        for comp in range(3):
            sides = []
            for s in (k, k + half):
                lanes = pl.ds(s * LANES, LANES)
                value = a[3, comp, :, strip(s)]
                out[comp, :, lanes] = value
                rest = value - keep * coarse[comp, :, lanes]
                detail[comp, :, lanes] = rest
                sides.append(pair_mean(rest, sub, lane))
            means.append(folded(*sides, lane))
        sides = [pair_mean(field[:, pl.ds(s * LANES, LANES)], sub, lane) for s in (k, k + half)]
        lanes = pl.ds(k * LANES, LANES)
        message[0, :, lanes] = zipped(means[0], means[1], sub)
        message[1, :, lanes] = zipped(means[2], LORENTZ * folded(*sides, lane), sub)


def coarse_step(bufs, field, tiles_of, strips, group):
    one, two, three = bufs
    length = FINE_STEPS * TIME_STEP
    run = functools.partial(stage, base=one, field=field, shift=2, cell=2.0, strips=strips, group=group)
    run(two, one, weight=1.0, length=length / 3.0, tiles=tiles_of(0))
    run(three, two, weight=1.0, length=length / 2.0, tiles=tiles_of(1))
    run(one, three, weight=1.0, length=length, tiles=tiles_of(2))


def coarse_kernel(count, strips, pos, state, field, sib, sib_a, sib_b, out, one, two, three, window):
    position = pos[0]
    side, near, _ = places(position)
    sub, lane = iotas()
    half = strips // 2

    def put(slot, ref, plane):
        for k in range(half):
            pairs = [pl.ds(s * LANES, LANES) for s in (k, k + half)]
            for comp in range(3):
                means = [pair_mean(ref[comp, :, lanes], sub, lane) for lanes in pairs]
                one[slot, comp, :, strip(k)] = folded(*means, lane)
            means = [pair_mean(plane[:, lanes], sub, lane) for lanes in pairs]
            window[slot, :, pl.ds(k * LANES, LANES)] = LORENTZ * folded(*means, lane)

    put(1, state, field)
    put(1 + side, sib, sib.at[3])
    for ref, sign in ((sib_a, 1), (sib_b, -1)):

        @pl.when(sign * near + side == -side)
        def _(ref=ref):
            put(1 - side, ref, ref.at[3])

    flip_field(window, position, count, 1)
    flip_state(one, position, count, 1)
    guards(one, range(3), 2, half)
    coarse_step((one, two, three), window, lambda n: range(3) if n < 2 else (1,), half, GROUP)
    for k in range(half):
        for comp in range(3):
            for s, value in zip((k, k + half), unfolded(one[1, comp, :, strip(k)], lane)):
                out[comp, :, pl.ds(s * LANES, LANES)] = value


def powers_kernel(
    count, strips, pos, own, sib, near_a, sib_a, near_b, sib_b, far_a, far_sa, far_b, far_sb, fifth,
    *refs,
):
    outs, (one, two, three, window) = refs[:3], refs[3:]
    position = pos[0]
    side, near, far = places(position)
    sub, lane = iotas()
    half = strips // 2
    arrived = (
        (own, 0), (sib, side), (near_a, near), (sib_a, near + side), (near_b, -near),
        (sib_b, side - near), (far_a, far), (far_sa, far + side), (far_b, -far),
        (far_sb, side - far), (fifth, -5 * side),
    )
    for ref, offset in arrived:
        slot = 5 + offset
        for k in range(half):
            lanes = pl.ds(k * LANES, LANES)
            height, east = unzipped(ref[0, :, lanes], sub)
            north, plane = unzipped(ref[1, :, lanes], sub)
            one[slot, 0, :, strip(k)] = height
            one[slot, 1, :, strip(k)] = east
            one[slot, 2, :, strip(k)] = north
            window[slot, :, lanes] = plane
    flip_field(window, position, count, 5)
    flip_state(one, position, count, 5)
    guards(one, range(11), 2, half)
    for s in range(6):

        def tiles_of(n, s=s):
            reach = -(-2 * (18 - 3 * s - n - 1) // ROWS)
            return range(5 - reach, 6 + reach)

        coarse_step((one, two, three), window, tiles_of, half, 4)
        out = outs[s // 2]
        for k in range(half):
            lanes = pl.ds(k * LANES, LANES)
            height, east, north = [one[5, comp, :, strip(k)] for comp in range(3)]
            out[s % 2, :, lanes] = zipped(height, east, sub)
            if s % 2 == 0:
                out[2, :, lanes] = north
            else:
                out[2, :, lanes] = zipped(out[2, :, lanes], north, sub)


def final_kernel(strips, pos, own, other, detail, anchor, out):
    sub, lane = iotas()
    half = strips // 2
    first = pos[1] == 0
    for k in range(half):
        lanes = pl.ds(k * LANES, LANES)
        height, east = unzipped(own[0, :, lanes] + other[1, :, lanes], sub)
        north = unzipped(own[2, :, lanes], sub)[0] + unzipped(other[2, :, lanes], sub)[1]
        for comp, value in enumerate((height, east, north)):
            for s, part in zip((k, k + half), unfolded(value, lane)):
                wide = pl.ds(s * LANES, LANES)
                total = part + detail[comp, :, wide]
                out[comp, :, wide] = jnp.where(first, anchor[comp, :, wide], total)


def call(kernel, outs, buffers, name, *args):
    return pl.pallas_call(
        kernel,
        out_shape=outs,
        in_specs=[SMEM] + [VMEM] * (len(args) - 1),
        out_specs=[VMEM] * len(outs),
        scratch_shapes=buffers,
        compiler_params=pltpu.CompilerParams(vmem_limit_bytes=48 * 1024 * 1024),
        name=name,
    )(*args)


def swap(block, partner):
    slices, count = lax.axis_size("tm"), lax.axis_size("space")
    pairs = [(i, partner(i)) for i in range(count)]
    pairs = [(i, j) for i, j in pairs if 0 <= j < count]
    return lax.ppermute(block, "space", pairs)


def later(block, distance):
    slices = lax.axis_size("tm")
    return lax.ppermute(block, "tm", [(m, m + distance) for m in range(slices - distance)])


def sibling(i):
    return i + 1 - 2 * (i % 2)


def near_odd(i):
    return i + (2 if (i // 2) % 2 == 1 else -2)


def near_even(i):
    return i - (2 if (i // 2) % 2 == 1 else -2)


def far_odd(i):
    return i + (4 if (i // 4) % 2 == 1 else -4)


def far_even(i):
    return i - (4 if (i // 4) % 2 == 1 else -4)


def third(i):
    return i - 3 if i % 2 == 0 else i + 3


def fifth(i):
    return i - 5 if i % 2 == 0 else i + 5


def body(start_state, vertical_field):
    state = start_state[0]
    cols = state.shape[2]
    strips = cols // LANES
    count = lax.axis_size("space")
    pos = jnp.stack([lax.axis_index("space"), lax.axis_index("tm")]).astype(jnp.int32)
    shape = lambda *dims: jax.ShapeDtypeStruct(dims, jnp.float32)
    tile = shape(3, ROWS, cols)
    buf = lambda tiles, wide: pltpu.VMEM((tiles, 3, ROWS, wide + 2 * LANES), jnp.float32)
    plane = lambda tiles, wide: pltpu.VMEM((tiles, ROWS, wide), jnp.float32)

    sent = jnp.concatenate([state, vertical_field[None]], axis=0)
    sib = swap(sent, sibling)
    b = swap(sent, near_even)
    q = swap(sent, third)
    a = swap(sent, near_odd)
    sib_b, sib_a = swap(b, sibling), swap(a, sibling)
    (coarse_end,) = call(
        functools.partial(coarse_kernel, count, strips),
        [tile],
        [buf(3, cols // 2)] * 3 + [plane(3, cols // 2)],
        "coarse",
        pos, state, vertical_field, sib, sib_a, sib_b,
    )
    fine_end, detail, message = call(
        functools.partial(fine_kernel, count, strips),
        [tile, tile, shape(2, ROWS, cols // 2)],
        [buf(7, cols), buf(7, cols), plane(7, cols)],
        "fine",
        pos, state, vertical_field, a, b, q, sib, sib_a, sib_b, coarse_end,
    )
    arrived = later(detail, 1)
    sib = swap(message, sibling)
    b = swap(message, near_even)
    d = swap(message, far_even)
    q = swap(message, fifth)
    c = swap(message, far_odd)
    a = swap(message, near_odd)
    sib_b, sib_d, sib_c, sib_a = [swap(x, sibling) for x in (b, d, c, a)]
    powers = call(
        functools.partial(powers_kernel, count, strips),
        [shape(3, ROWS, cols // 2)] * 3,
        [buf(11, cols // 2)] * 3 + [plane(11, cols // 2)],
        "powers",
        pos, message, sib, a, sib_a, b, sib_b, c, sib_c, d, sib_d, q,
    )
    own = sum(later(x, 2 * d + 2) for d, x in enumerate(powers))
    other = later(own, 1)
    (new_start,) = call(
        functools.partial(final_kernel, strips),
        [tile],
        [],
        "final",
        pos, own, other, arrived, state,
    )
    return (new_start[None], fine_end[None], coarse_end[None])


def solution(mesh):
    in_specs = (P("tm", None, "space", None), P("space", None))
    out_specs = (
        P("tm", None, "space", None),
        P("tm", None, "space", None),
        P("tm", None, "space", None),
    )
    return jax.shard_map(body, mesh=mesh, in_specs=in_specs, out_specs=out_specs, check_vma=False)
```

```python
import functools

import jax
import jax.numpy as jnp
from jax import lax
from jax.experimental import pallas as pl
from jax.experimental.pallas import tpu as pltpu
from jax.sharding import PartitionSpec as P

FINE_STEPS = 8
LORENTZ = 0.3
FRICTION = 0.01
TIME_STEP = 0.28
ROWS = 8
LANES = 128

ALPHA = 0.6265382932707997
QUAD_A = 0.3734617067292003
QUAD_B = 0.2660119396638869

VMEM = pl.BlockSpec(memory_space=pltpu.VMEM)
SMEM = pl.BlockSpec(memory_space=pltpu.SMEM)


def iotas():
    sub = lax.broadcasted_iota(jnp.int32, (ROWS, LANES), 0)
    lane = lax.broadcasted_iota(jnp.int32, (ROWS, LANES), 1)
    return sub, lane


def guard_strips(firsts, lasts, shift, lane):
    even = lane % 2 == 0
    result = []
    for sign, first, last in zip((1.0, -1.0), firsts, lasts):
        low = sign * pltpu.roll(first, LANES - shift, 1)
        high = sign * pltpu.roll(last, shift, 1)
        if shift == 2:
            low = jnp.where(even, low, pltpu.roll(last, 1, 1))
            high = jnp.where(even, pltpu.roll(first, LANES - 1, 1), high)
        result.append((low, high))
    return result


def set_guards(buf, blocks, shift):
    strips = buf.shape[1] - 2
    _, lane = iotas()

    def block(t, carry):
        rows = pl.ds(pl.multiple_of(t * ROWS, ROWS), ROWS)
        firsts = [buf[comp, 1, rows, :] for comp in (0, 2)]
        lasts = [buf[comp, strips, rows, :] for comp in (0, 2)]
        for comp, (low, high) in zip((0, 2), guard_strips(firsts, lasts, shift, lane)):
            buf[comp, 0, rows, :] = low
            buf[comp, strips + 1, rows, :] = high
        return carry

    lax.fori_loop(0, blocks, block, 0)


def stage(dst, src, base, weight, length, field, start, count, shift, cell, unroll):
    factor = length / (2.0 * cell)
    drag = FRICTION * length
    strips = src.shape[1] - 2
    _, lane = iotas()
    lanes_high = lane >= LANES - shift
    lanes_low = lane < shift
    step = ROWS * unroll

    def block(n, carry):
        for u in range(unroll):
            r = start + n * step + ROWS * u
            rows, above, below = pl.ds(r, ROWS), pl.ds(r - shift, ROWS), pl.ds(r + shift, ROWS)
            firsts = lasts = None
            for k in range(1, strips + 1):
                height, east, north = [src[comp, k, rows, :] for comp in range(3)]

                def row_diff(comp):
                    return src[comp, k, below, :] - src[comp, k, above, :]

                def col_diff(comp, centre):
                    before = jnp.where(lanes_high, src[comp, k - 1, rows, :], centre)
                    after = jnp.where(lanes_low, src[comp, k + 1, rows, :], centre)
                    return pltpu.roll(after, LANES - shift, 1) - pltpu.roll(before, shift, 1)

                b = field[k - 1, rows, :]
                dx, dy = row_diff(0), col_diff(0, height)
                rise = row_diff(1) + col_diff(2, north)
                if base is src:
                    new_height = weight * height - factor * rise
                    new_east = (weight - drag) * east + factor * (b * dy - dx)
                    new_north = (weight - drag) * north - factor * (b * dx + dy)
                else:
                    old = [base[comp, k, rows, :] for comp in range(3)]
                    new_height = old[0] - factor * rise
                    new_east = old[1] - drag * east + factor * (b * dy - dx)
                    new_north = old[2] - drag * north - factor * (b * dx + dy)
                dst[0, k, rows, :] = new_height
                dst[1, k, rows, :] = new_east
                dst[2, k, rows, :] = new_north
                if k == 1:
                    firsts = (new_height, new_north)
                if k == strips:
                    lasts = (new_height, new_north)
            for comp, (low, high) in zip((0, 2), guard_strips(firsts, lasts, shift, lane)):
                dst[comp, 0, rows, :] = low
                dst[comp, strips + 1, rows, :] = high
        return carry

    lax.fori_loop(0, lax.div(count + step - 1, step), block, 0)


def pair_mean(x, sub, lane):
    x = x + jnp.where(sub % 2 == 0, pltpu.roll(x, ROWS - 1, 0), pltpu.roll(x, 1, 0))
    x = x + jnp.where(lane % 2 == 0, pltpu.roll(x, LANES - 1, 1), pltpu.roll(x, 1, 1))
    return 0.25 * x


def flip_tiles(position, count, halo, copy_row):
    low = jnp.maximum(halo - position, 0)
    high = jnp.maximum(position + halo - (count - 1), 0)
    wall_low = ROWS * (halo - position)
    wall_high = ROWS * (halo - position + count)

    def fill_low(q, carry):
        for r in range(ROWS):
            copy_row(wall_low - 1 - ROWS * q - r, wall_low + ROWS * q + r)
        return carry

    def fill_high(q, carry):
        for r in range(ROWS):
            copy_row(wall_high + ROWS * q + r, wall_high - 1 - ROWS * q - r)
        return carry

    lax.fori_loop(0, low, fill_low, 0)
    lax.fori_loop(0, high, fill_high, 0)


def flip(buf, field, position, count, halo):
    strips = field.shape[0]

    def copy_row(to, source):
        to, source = pl.ds(to, 1), pl.ds(source, 1)
        for k in range(strips):
            for comp, sign in ((0, 1.0), (1, -1.0), (2, 1.0)):
                buf[comp, k + 1, to, :] = sign * buf[comp, k + 1, source, :]
            field[k, to, :] = -field[k, source, :]

    flip_tiles(position, count, halo, copy_row)


def tile_rows(slot):
    return pl.ds(slot * ROWS if isinstance(slot, int) else pl.multiple_of(slot * ROWS, ROWS), ROWS)


def lanes_of(k):
    return pl.ds(k * LANES, LANES)


def folded(left, right, lane):
    return jnp.where(lane % 2 == 0, left, right)


def unfolded(x, lane):
    left = jnp.where(lane % 2 == 0, x, pltpu.roll(x, 1, 1))
    right = jnp.where(lane % 2 == 1, x, pltpu.roll(x, LANES - 1, 1))
    return left, right


def zipped(even, odd, sub):
    return jnp.where(sub % 2 == 0, even, odd)


def unzipped(x, sub):
    even = jnp.where(sub % 2 == 0, x, pltpu.roll(x, 1, 0))
    odd = jnp.where(sub % 2 == 1, x, pltpu.roll(x, ROWS - 1, 0))
    return even, odd


def places(position):
    core = lax.rem(position, 2)
    chip = lax.div(position, 2)
    side = 1 - 2 * core
    near = 2 * (2 * lax.rem(chip, 2) - 1)
    far = 4 * (2 * lax.rem(lax.div(chip, 2), 2) - 1)
    return side, near, far


def fine_kernel(
    count, strips, pos, state, field, near_a, near_b, third, sib, sib_a, sib_b, coarse,
    out, detail, message, one, two, window,
):
    position = pos[0]
    side, near, _ = places(position)
    arrived = (
        (near_a, near), (near_b, -near), (third, -3 * side),
        (sib, side), (sib_a, near + side), (sib_b, side - near),
    )
    middle = tile_rows(3)
    for k in range(strips):
        window[k, middle, :] = LORENTZ * field[:, lanes_of(k)]
        for comp in range(3):
            one[comp, k + 1, middle, :] = state[comp, :, lanes_of(k)]
    for ref, offset in arrived:
        rows = tile_rows(3 + offset)
        for k in range(strips):
            window[k, rows, :] = LORENTZ * ref[3, :, lanes_of(k)]
            for comp in range(3):
                one[comp, k + 1, rows, :] = ref[comp, :, lanes_of(k)]
    flip(one, window, position, count, 3)
    set_guards(one, 7, 1)

    run = functools.partial(stage, field=window, shift=1, cell=1.0, unroll=2)

    def two_steps(j, carry):
        a, b = one, two
        for half in range(2):
            s = 6 * j + 3 * half + 1
            run(b, a, a, QUAD_A, QUAD_B * TIME_STEP, start=s, count=56 - 2 * s)
            run(a, b, a, 1.0, TIME_STEP, start=s + 1, count=54 - 2 * s)
            run(b, a, a, 1.0, ALPHA * TIME_STEP, start=s + 2, count=52 - 2 * s)
            a, b = b, a
        return carry

    lax.fori_loop(0, FINE_STEPS // 2, two_steps, 0)

    sub, lane = iotas()
    keep = jnp.where(pos[1] == 0, 0.0, 1.0)
    half = strips // 2
    for k in range(half):
        means = []
        for comp in range(3):
            sides = []
            both = unfolded(coarse[comp, :, lanes_of(k)], lane)
            for s, less in zip((k, k + half), both):
                value = one[comp, s + 1, middle, :]
                out[comp, :, lanes_of(s)] = value
                rest = value - keep * less
                detail[comp, :, lanes_of(s)] = rest
                sides.append(pair_mean(rest, sub, lane))
            means.append(folded(*sides, lane))
        sides = [pair_mean(field[:, lanes_of(s)], sub, lane) for s in (k, k + half)]
        message[0, :, lanes_of(k)] = zipped(means[0], means[1], sub)
        message[1, :, lanes_of(k)] = zipped(means[2], LORENTZ * folded(*sides, lane), sub)


def coarse_step(bufs, field, start, count, unroll):
    one, two, three = bufs
    length = FINE_STEPS * TIME_STEP
    run = functools.partial(stage, base=one, weight=1.0, field=field, shift=2, cell=2.0, unroll=unroll)
    run(two, one, length=length / 3.0, start=start, count=count)
    run(three, two, length=length / 2.0, start=start + 2, count=count - 4)
    run(one, three, length=length, start=start + 4, count=count - 8)


def coarse_kernel(
    count, strips, pos, state, field, sib, sib_a, sib_b, out, short, one, two, three, window
):
    position = pos[0]
    side, near, _ = places(position)
    sub, lane = iotas()
    half = strips // 2

    def put(slot, ref, plane):
        rows = tile_rows(slot)
        for k in range(half):
            pairs = [lanes_of(s) for s in (k, k + half)]
            for comp in range(3):
                means = [pair_mean(ref[comp, :, lanes], sub, lane) for lanes in pairs]
                one[comp, k + 1, rows, :] = folded(*means, lane)
            means = [pair_mean(plane[:, lanes], sub, lane) for lanes in pairs]
            window[k, rows, :] = LORENTZ * folded(*means, lane)

    put(1, state, field)
    put(1 + side, sib, sib.at[3])
    for ref, sign in ((sib_a, 1), (sib_b, -1)):

        @pl.when(sign * near + side == -side)
        def _(ref=ref):
            put(1 - side, ref, ref.at[3])

    flip(one, window, position, count, 1)
    set_guards(one, 3, 2)
    zero = lax.div(position, count)
    coarse_step((one, two, three), window, zero + 4, 16, 2)
    for k in range(half):
        for comp in range(3):
            value = one[comp, k + 1, tile_rows(1), :]
            short[comp, :, lanes_of(k)] = value
            for s, part in zip((k, k + half), unfolded(value, lane)):
                out[comp, :, lanes_of(s)] = part


def powers_kernel(
    count, strips, pos, own, sib, near_a, near_b, far_a, far_b, fifth, others, *refs
):
    outs, (one, two, three, window) = refs[:3], refs[3:]
    position = pos[0]
    side, near, far = places(position)
    sub, lane = iotas()
    half = strips // 2
    arrived = (
        (own, 0, 0), (sib, 0, side), (near_a, 0, near), (near_b, 0, -near), (far_a, 0, far),
        (far_b, 0, -far), (fifth, 0, -5 * side), (others, 0, near + side),
        (others, 2, side - near), (others, 4, far + side), (others, 6, side - far),
    )
    for ref, at, offset in arrived:
        rows = tile_rows(5 + offset)
        for k in range(half):
            height, east = unzipped(ref[at, :, lanes_of(k)], sub)
            north, plane = unzipped(ref[at + 1, :, lanes_of(k)], sub)
            one[0, k + 1, rows, :] = height
            one[1, k + 1, rows, :] = east
            one[2, k + 1, rows, :] = north
            window[k, rows, :] = plane
    flip(one, window, position, count, 5)
    set_guards(one, 11, 2)
    middle = tile_rows(5)

    def two_steps(j, carry):
        for odd in range(2):
            s = 6 * j + 3 * odd + 1
            coarse_step((one, two, three), window, 4 + 2 * s, 80 - 4 * s, 4)
            for d, out in enumerate(outs):

                @pl.when(j == d)
                def _(out=out, odd=odd):
                    for k in range(half):
                        height, east, north = [one[comp, k + 1, middle, :] for comp in range(3)]
                        out[odd, :, lanes_of(k)] = zipped(height, east, sub)
                        if odd == 0:
                            out[2, :, lanes_of(k)] = north
                        else:
                            out[2, :, lanes_of(k)] = zipped(out[2, :, lanes_of(k)], north, sub)

        return carry

    lax.fori_loop(0, 3, two_steps, 0)


def final_kernel(strips, pos, own, other, detail, anchor, out):
    sub, lane = iotas()
    half = strips // 2
    first = pos[1] == 0
    for k in range(half):
        lanes = pl.ds(k * LANES, LANES)
        height, east = unzipped(own[0, :, lanes] + other[1, :, lanes], sub)
        north = unzipped(own[2, :, lanes], sub)[0] + unzipped(other[2, :, lanes], sub)[1]
        for comp, value in enumerate((height, east, north)):
            for s, part in zip((k, k + half), unfolded(value, lane)):
                wide = pl.ds(s * LANES, LANES)
                total = part + detail[comp, :, wide]
                out[comp, :, wide] = jnp.where(first, anchor[comp, :, wide], total)


def call(kernel, outs, buffers, name, *args):
    return pl.pallas_call(
        kernel,
        out_shape=outs,
        in_specs=[SMEM] + [VMEM] * (len(args) - 1),
        out_specs=[VMEM] * len(outs),
        scratch_shapes=buffers,
        compiler_params=pltpu.CompilerParams(vmem_limit_bytes=48 * 1024 * 1024),
        name=name,
    )(*args)


def swap(block, partner):
    slices, count = lax.axis_size("tm"), lax.axis_size("space")
    pairs = [(i, partner(i)) for i in range(count)]
    pairs = [(i, j) for i, j in pairs if 0 <= j < count]
    return lax.ppermute(block, "space", pairs)


def later(block, distance):
    slices = lax.axis_size("tm")
    return lax.ppermute(block, "tm", [(m, m + distance) for m in range(slices - distance)])


def sibling(i):
    return i + 1 - 2 * (i % 2)


def near_odd(i):
    return i + (2 if (i // 2) % 2 == 1 else -2)


def near_even(i):
    return i - (2 if (i // 2) % 2 == 1 else -2)


def far_odd(i):
    return i + (4 if (i // 4) % 2 == 1 else -4)


def far_even(i):
    return i - (4 if (i // 4) % 2 == 1 else -4)


def third(i):
    return i - 3 if i % 2 == 0 else i + 3


def fifth(i):
    return i - 5 if i % 2 == 0 else i + 5


def body(start_state, vertical_field):
    state = start_state[0]
    cols = state.shape[2]
    strips = cols // LANES
    count = lax.axis_size("space")
    pos = jnp.stack([lax.axis_index("space"), lax.axis_index("tm")]).astype(jnp.int32)
    shape = lambda *dims: jax.ShapeDtypeStruct(dims, jnp.float32)
    tile = shape(3, ROWS, cols)

    def room(tiles, strips, spare):
        rows = (tiles + spare) * ROWS
        state = pltpu.VMEM((3, strips + 2, rows, LANES), jnp.float32)
        return state, pltpu.VMEM((strips, rows, LANES), jnp.float32)

    sent = jnp.concatenate([state, vertical_field[None]], axis=0)
    sib = swap(sent, sibling)
    b = swap(sent, near_even)
    q = swap(sent, third)
    a = swap(sent, near_odd)
    a, b, q = lax.optimization_barrier((a, b, q))
    sib_b, sib_a = swap(b, sibling), swap(a, sibling)
    big, field = room(3, strips // 2, 2)
    coarse_end, short = call(
        functools.partial(coarse_kernel, count, strips),
        [tile, shape(3, ROWS, cols // 2)],
        [big, big, big, field],
        "coarse",
        pos, state, vertical_field, sib, sib_a, sib_b,
    )
    big, field = room(7, strips, 2)
    fine_end, detail, message = call(
        functools.partial(fine_kernel, count, strips),
        [tile, tile, shape(2, ROWS, cols // 2)],
        [big, big, field],
        "fine",
        pos, state, vertical_field, a, b, q, sib, sib_a, sib_b, short,
    )
    arrived = later(detail, 1)
    sib = swap(message, sibling)
    b = swap(message, near_even)
    d = swap(message, far_even)
    q = swap(message, fifth)
    c = swap(message, far_odd)
    a = swap(message, near_odd)
    a, b, c, d, q, arrived = lax.optimization_barrier((a, b, c, d, q, arrived))
    others = swap(jnp.concatenate([a, b, c, d], axis=0), sibling)
    big, field = room(11, strips // 2, 4)
    powers = call(
        functools.partial(powers_kernel, count, strips),
        [shape(3, ROWS, cols // 2)] * 3,
        [big, big, big, field],
        "powers",
        pos, message, sib, a, b, c, d, q, others,
    )
    own = sum(later(x, 2 * d + 2) for d, x in enumerate(powers))
    other = later(own, 1)
    (new_start,) = call(
        functools.partial(final_kernel, strips),
        [tile],
        [],
        "final",
        pos, own, other, arrived, state,
    )
    return (new_start[None], fine_end[None], coarse_end[None])


def solution(mesh):
    in_specs = (P("tm", None, "space", None), P("space", None))
    out_specs = (
        P("tm", None, "space", None),
        P("tm", None, "space", None),
        P("tm", None, "space", None),
    )
    return jax.shard_map(body, mesh=mesh, in_specs=in_specs, out_specs=out_specs, check_vma=False)
```

```python
import functools

import jax
import jax.numpy as jnp
from jax import lax
from jax.experimental import pallas as pl
from jax.experimental.pallas import tpu as pltpu
from jax.sharding import PartitionSpec as P

FINE_STEPS = 8
LORENTZ = 0.3
FRICTION = 0.01
TIME_STEP = 0.28
ROWS = 8
LANES = 128
GROUP = 8

ALPHA = 0.6265382932707997
QUAD_A = 0.3734617067292003
QUAD_B = 0.2660119396638869

VMEM = pl.BlockSpec(memory_space=pltpu.VMEM)
SMEM = pl.BlockSpec(memory_space=pltpu.SMEM)


def iotas():
    sub = lax.broadcasted_iota(jnp.int32, (ROWS, LANES), 0)
    lane = lax.broadcasted_iota(jnp.int32, (ROWS, LANES), 1)
    return sub, lane


def strip(k):
    start = LANES + k * LANES
    return pl.ds(start if isinstance(start, int) else pl.multiple_of(start, LANES), LANES)


def guards(buf, tiles, shift, strips):
    _, lane = iotas()
    even = lane % 2 == 0
    for t in tiles:
        for comp, sign in ((0, 1.0), (2, -1.0)):
            first = buf[t, comp, :, strip(0)]
            last = buf[t, comp, :, strip(strips - 1)]
            low = sign * pltpu.roll(first, LANES - shift, 1)
            high = sign * pltpu.roll(last, shift, 1)
            if shift == 2:
                low = jnp.where(even, low, pltpu.roll(last, 1, 1))
                high = jnp.where(even, pltpu.roll(first, LANES - 1, 1), high)
            buf[t, comp, :, strip(-1)] = low
            buf[t, comp, :, strip(strips)] = high


def stage(dst, src, base, weight, length, field, tiles, shift, cell, strips, group):
    factor = length / (2.0 * cell)
    drag = FRICTION * length
    sub, lane = iotas()
    rows_high = sub >= ROWS - shift
    rows_low = sub < shift
    lanes_high = lane >= LANES - shift
    lanes_low = lane < shift
    slots = dst.shape[0]
    group = min(group, strips)

    def block(g, carry):
        for j in range(group):
            k = g * group + j
            here = strip(k)
            cache = {}

            def get(comp, t):
                t = min(max(t, 0), slots - 1)
                if (comp, t) not in cache:
                    cache[comp, t] = src[t, comp, :, here]
                return cache[comp, t]

            for t in tiles:
                height, east, north = get(0, t), get(1, t), get(2, t)

                def row_diff(comp, centre):
                    before = jnp.where(rows_high, get(comp, t - 1), centre)
                    after = jnp.where(rows_low, get(comp, t + 1), centre)
                    return pltpu.roll(after, ROWS - shift, 0) - pltpu.roll(before, shift, 0)

                def col_diff(comp, centre):
                    before = jnp.where(lanes_high, src[t, comp, :, strip(k - 1)], centre)
                    after = jnp.where(lanes_low, src[t, comp, :, strip(k + 1)], centre)
                    return pltpu.roll(after, LANES - shift, 1) - pltpu.roll(before, shift, 1)

                b = field[t, :, pl.ds(here.start - LANES, LANES)]
                dx, dy = row_diff(0, height), col_diff(0, height)
                rise = row_diff(1, east) + col_diff(2, north)
                if base is src:
                    new_height = weight * height - factor * rise
                    new_east = (weight - drag) * east + factor * (b * dy - dx)
                    new_north = (weight - drag) * north - factor * (b * dx + dy)
                else:
                    old = [base[t, comp, :, here] for comp in range(3)]
                    if weight != 1.0:
                        old = [weight * o for o in old]
                    new_height = old[0] - factor * rise
                    new_east = old[1] - drag * east + factor * (b * dy - dx)
                    new_north = old[2] - drag * north - factor * (b * dx + dy)
                dst[t, 0, :, here] = new_height
                dst[t, 1, :, here] = new_east
                dst[t, 2, :, here] = new_north
        return carry

    lax.fori_loop(0, strips // group, block, 0)
    guards(dst, tiles, shift, strips)


def pair_mean(x, sub, lane):
    x = x + jnp.where(sub % 2 == 0, pltpu.roll(x, ROWS - 1, 0), pltpu.roll(x, 1, 0))
    x = x + jnp.where(lane % 2 == 0, pltpu.roll(x, LANES - 1, 1), pltpu.roll(x, 1, 1))
    return 0.25 * x


def flip_tiles(position, count, halo, first, copy_row):
    low = jnp.maximum(halo - position, 0)
    high = jnp.maximum(position + halo - (count - 1), 0)

    def fill_low(q, carry):
        for r in range(ROWS):
            copy_row(first + halo - position - 1 - q, ROWS - 1 - r, first + halo - position + q, r)
        return carry

    def fill_high(q, carry):
        for r in range(ROWS):
            copy_row(
                first + count + q - position + halo,
                ROWS - 1 - r,
                first + count - 1 - q - position + halo,
                r,
            )
        return carry

    lax.fori_loop(0, low, fill_low, 0)
    lax.fori_loop(0, high, fill_high, 0)


def flip_state(buf, position, count, halo, first=0):
    cols = pl.ds(LANES, buf.shape[3] - 2 * LANES)

    def copy_row(t_to, r_to, t_from, r_from):
        for comp, sign in ((0, 1.0), (1, -1.0), (2, 1.0)):
            buf[t_to, comp, pl.ds(r_to, 1), cols] = sign * buf[t_from, comp, pl.ds(r_from, 1), cols]

    flip_tiles(position, count, halo, first, copy_row)


def flip_field(field, position, count, halo):
    def copy_row(t_to, r_to, t_from, r_from):
        field[t_to, pl.ds(r_to, 1), :] = -field[t_from, pl.ds(r_from, 1), :]

    flip_tiles(position, count, halo, 0, copy_row)


def folded(left, right, lane):
    return jnp.where(lane % 2 == 0, left, right)


def unfolded(x, lane):
    left = jnp.where(lane % 2 == 0, x, pltpu.roll(x, 1, 1))
    right = jnp.where(lane % 2 == 1, x, pltpu.roll(x, LANES - 1, 1))
    return left, right


def zipped(even, odd, sub):
    return jnp.where(sub % 2 == 0, even, odd)


def unzipped(x, sub):
    even = jnp.where(sub % 2 == 0, x, pltpu.roll(x, 1, 0))
    odd = jnp.where(sub % 2 == 1, x, pltpu.roll(x, ROWS - 1, 0))
    return even, odd


def places(position):
    core = lax.rem(position, 2)
    chip = lax.div(position, 2)
    side = 1 - 2 * core
    near = 2 * (2 * lax.rem(chip, 2) - 1)
    far = 4 * (2 * lax.rem(lax.div(chip, 2), 2) - 1)
    return side, near, far


def fine_kernel(
    count, strips, pos, state, field, near_a, near_b, third, sib, sib_a, sib_b, coarse,
    out, detail, message, one, two, window,
):
    position = pos[0]
    side, near, _ = places(position)
    cols = pl.ds(LANES, strips * LANES)
    arrived = (
        (near_a, near), (near_b, -near), (third, -3 * side),
        (sib, side), (sib_a, near + side), (sib_b, side - near),
    )
    window[3] = LORENTZ * field[...]
    for comp in range(3):
        one[3, comp, :, cols] = state[comp]
    for ref, offset in arrived:
        slot = 3 + offset
        window[slot] = LORENTZ * ref[3]
        for comp in range(3):
            one[slot, comp, :, cols] = ref[comp]
    flip_field(window, position, count, 3)
    flip_state(one, position, count, 3)
    guards(one, range(7), 1, strips)

    run = functools.partial(stage, field=window, shift=1, cell=1.0, strips=strips, group=GROUP)
    a, b = one, two
    for reach, quads, lines in ((3, 3, 2), (2, 3, 2), (1, 2, 4)):
        tiles = range(3 - reach, 4 + reach)

        def quad(step, carry, a=a, b=b, tiles=tiles):
            run(b, a, a, QUAD_A, QUAD_B * TIME_STEP, tiles=tiles)
            run(a, b, a, 1.0, TIME_STEP, tiles=tiles)
            return carry

        lax.fori_loop(0, quads, quad, 0)
        for n in range(lines):
            if n == lines - 1:
                tiles = range(4 - reach, 3 + reach)
            run(b, a, a, 1.0, ALPHA * TIME_STEP, tiles=tiles)
            a, b = b, a

    sub, lane = iotas()
    keep = jnp.where(pos[1] == 0, 0.0, 1.0)
    half = strips // 2
    for k in range(half):
        means = []
        for comp in range(3):
            sides = []
            both = unfolded(coarse[comp, :, pl.ds(k * LANES, LANES)], lane)
            for s, less in zip((k, k + half), both):
                lanes = pl.ds(s * LANES, LANES)
                value = a[3, comp, :, strip(s)]
                out[comp, :, lanes] = value
                rest = value - keep * less
                detail[comp, :, lanes] = rest
                sides.append(pair_mean(rest, sub, lane))
            means.append(folded(*sides, lane))
        sides = [pair_mean(field[:, pl.ds(s * LANES, LANES)], sub, lane) for s in (k, k + half)]
        lanes = pl.ds(k * LANES, LANES)
        message[0, :, lanes] = zipped(means[0], means[1], sub)
        message[1, :, lanes] = zipped(means[2], LORENTZ * folded(*sides, lane), sub)


def coarse_step(bufs, field, tiles_of, strips, group):
    one, two, three = bufs
    length = FINE_STEPS * TIME_STEP
    run = functools.partial(stage, base=one, field=field, shift=2, cell=2.0, strips=strips, group=group)
    run(two, one, weight=1.0, length=length / 3.0, tiles=tiles_of(0))
    run(three, two, weight=1.0, length=length / 2.0, tiles=tiles_of(1))
    run(one, three, weight=1.0, length=length, tiles=tiles_of(2))


def coarse_kernel(
    count, strips, pos, state, field, sib, sib_a, sib_b, out, short, one, two, three, window
):
    position = pos[0]
    side, near, _ = places(position)
    sub, lane = iotas()
    half = strips // 2

    def put(slot, ref, plane):
        for k in range(half):
            pairs = [pl.ds(s * LANES, LANES) for s in (k, k + half)]
            for comp in range(3):
                means = [pair_mean(ref[comp, :, lanes], sub, lane) for lanes in pairs]
                one[slot, comp, :, strip(k)] = folded(*means, lane)
            means = [pair_mean(plane[:, lanes], sub, lane) for lanes in pairs]
            window[slot, :, pl.ds(k * LANES, LANES)] = LORENTZ * folded(*means, lane)

    put(1, state, field)
    put(1 + side, sib, sib.at[3])
    for ref, sign in ((sib_a, 1), (sib_b, -1)):

        @pl.when(sign * near + side == -side)
        def _(ref=ref):
            put(1 - side, ref, ref.at[3])

    flip_field(window, position, count, 1)
    flip_state(one, position, count, 1)
    guards(one, range(3), 2, half)
    coarse_step((one, two, three), window, lambda n: range(3) if n < 2 else (1,), half, GROUP)
    for k in range(half):
        for comp in range(3):
            value = one[1, comp, :, strip(k)]
            short[comp, :, pl.ds(k * LANES, LANES)] = value
            for s, part in zip((k, k + half), unfolded(value, lane)):
                out[comp, :, pl.ds(s * LANES, LANES)] = part


def powers_kernel(
    count, strips, pos, own, sib, near_a, near_b, far_a, far_b, fifth, others, *refs
):
    outs, (one, two, three, window) = refs[:3], refs[3:]
    position = pos[0]
    side, near, far = places(position)
    sub, lane = iotas()
    half = strips // 2
    arrived = (
        (own, 0, 0), (sib, 0, side), (near_a, 0, near), (near_b, 0, -near), (far_a, 0, far),
        (far_b, 0, -far), (fifth, 0, -5 * side), (others, 0, near + side),
        (others, 2, side - near), (others, 4, far + side), (others, 6, side - far),
    )
    for ref, at, offset in arrived:
        slot = 5 + offset
        for k in range(half):
            lanes = pl.ds(k * LANES, LANES)
            height, east = unzipped(ref[at, :, lanes], sub)
            north, plane = unzipped(ref[at + 1, :, lanes], sub)
            one[slot, 0, :, strip(k)] = height
            one[slot, 1, :, strip(k)] = east
            one[slot, 2, :, strip(k)] = north
            window[slot, :, lanes] = plane
    flip_field(window, position, count, 5)
    flip_state(one, position, count, 5)
    guards(one, range(11), 2, half)
    for s in range(6):

        def tiles_of(n, s=s):
            reach = -(-2 * (18 - 3 * s - n - 1) // ROWS)
            return range(5 - reach, 6 + reach)

        coarse_step((one, two, three), window, tiles_of, half, 4)
        out = outs[s // 2]
        for k in range(half):
            lanes = pl.ds(k * LANES, LANES)
            height, east, north = [one[5, comp, :, strip(k)] for comp in range(3)]
            out[s % 2, :, lanes] = zipped(height, east, sub)
            if s % 2 == 0:
                out[2, :, lanes] = north
            else:
                out[2, :, lanes] = zipped(out[2, :, lanes], north, sub)


def final_kernel(strips, pos, own, other, detail, anchor, out):
    sub, lane = iotas()
    half = strips // 2
    first = pos[1] == 0
    for k in range(half):
        lanes = pl.ds(k * LANES, LANES)
        height, east = unzipped(own[0, :, lanes] + other[0, :, lanes], sub)
        north = unzipped(own[2, :, lanes], sub)[0] + unzipped(other[1, :, lanes], sub)[1]
        for comp, value in enumerate((height, east, north)):
            for s, part in zip((k, k + half), unfolded(value, lane)):
                wide = pl.ds(s * LANES, LANES)
                total = part + detail[comp, :, wide]
                out[comp, :, wide] = jnp.where(first, anchor[comp, :, wide], total)


def call(kernel, outs, buffers, name, *args):
    return pl.pallas_call(
        kernel,
        out_shape=outs,
        in_specs=[SMEM] + [VMEM] * (len(args) - 1),
        out_specs=[VMEM] * len(outs),
        scratch_shapes=buffers,
        compiler_params=pltpu.CompilerParams(vmem_limit_bytes=48 * 1024 * 1024),
        name=name,
    )(*args)


def swap(block, partner):
    slices, count = lax.axis_size("tm"), lax.axis_size("space")
    pairs = [(i, partner(i)) for i in range(count)]
    pairs = [(i, j) for i, j in pairs if 0 <= j < count]
    return lax.ppermute(block, "space", pairs)


def later(block, distance):
    slices = lax.axis_size("tm")
    return lax.ppermute(block, "tm", [(m, m + distance) for m in range(slices - distance)])


def in_two_legs(block):
    slices, count = lax.axis_size("tm"), lax.axis_size("space")
    run = min(8, count // 2)
    legs = [], []
    for m in range(slices - 1):
        for i in range(count):
            y, upper = divmod(m, 2)
            group, low = divmod(i // 2, run)
            way = 1 if i % 2 == 0 else -1
            upper, low = divmod((upper * run + low + way * (run // 2)) % (2 * run), run)
            stop = (2 * y + upper) * count + 2 * (group * run + low) + i % 2
            legs[0].append((m * count + i, stop))
            legs[1].append((stop, (m + 1) * count + i))
    for leg in legs:
        block = lax.ppermute(block, ("tm", "space"), leg)
    return block


def sibling(i):
    return i + 1 - 2 * (i % 2)


def near_odd(i):
    return i + (2 if (i // 2) % 2 == 1 else -2)


def near_even(i):
    return i - (2 if (i // 2) % 2 == 1 else -2)


def far_odd(i):
    return i + (4 if (i // 4) % 2 == 1 else -4)


def far_even(i):
    return i - (4 if (i // 4) % 2 == 1 else -4)


def third(i):
    return i - 3 if i % 2 == 0 else i + 3


def fifth(i):
    return i - 5 if i % 2 == 0 else i + 5


def body(start_state, vertical_field):
    state = start_state[0]
    cols = state.shape[2]
    strips = cols // LANES
    count = lax.axis_size("space")
    pos = jnp.stack([lax.axis_index("space"), lax.axis_index("tm")]).astype(jnp.int32)
    shape = lambda *dims: jax.ShapeDtypeStruct(dims, jnp.float32)
    tile = shape(3, ROWS, cols)
    buf = lambda tiles, wide: pltpu.VMEM((tiles, 3, ROWS, wide + 2 * LANES), jnp.float32)
    plane = lambda tiles, wide: pltpu.VMEM((tiles, ROWS, wide), jnp.float32)

    sent = jnp.concatenate([state, vertical_field[None]], axis=0)
    sib = swap(sent, sibling)
    b = swap(sent, near_even)
    q = swap(sent, third)
    a = swap(sent, near_odd)
    a, b, q = lax.optimization_barrier((a, b, q))
    sib_b, sib_a = swap(b, sibling), swap(a, sibling)
    coarse_end, short = call(
        functools.partial(coarse_kernel, count, strips),
        [tile, shape(3, ROWS, cols // 2)],
        [buf(3, cols // 2)] * 3 + [plane(3, cols // 2)],
        "coarse",
        pos, state, vertical_field, sib, sib_a, sib_b,
    )
    fine_end, detail, message = call(
        functools.partial(fine_kernel, count, strips),
        [tile, tile, shape(2, ROWS, cols // 2)],
        [buf(7, cols), buf(7, cols), plane(7, cols)],
        "fine",
        pos, state, vertical_field, a, b, q, sib, sib_a, sib_b, short,
    )
    arrived = in_two_legs(detail)
    sib = swap(message, sibling)
    b = swap(message, near_even)
    d = swap(message, far_even)
    q = swap(message, fifth)
    c = swap(message, far_odd)
    a = swap(message, near_odd)
    a, b, c, d, q = lax.optimization_barrier((a, b, c, d, q))
    others = swap(jnp.concatenate([a, b, c, d], axis=0), sibling)
    powers = call(
        functools.partial(powers_kernel, count, strips),
        [shape(3, ROWS, cols // 2)] * 3,
        [buf(11, cols // 2)] * 3 + [plane(11, cols // 2)],
        "powers",
        pos, message, sib, a, b, c, d, q, others,
    )
    own = sum(later(x, 2 * d + 2) for d, x in enumerate(powers))
    other = later(own[1:], 1)
    (new_start,) = call(
        functools.partial(final_kernel, strips),
        [tile],
        [],
        "final",
        pos, own, other, arrived, state,
    )
    return (new_start[None], fine_end[None], coarse_end[None])


def solution(mesh):
    in_specs = (P("tm", None, "space", None), P("space", None))
    out_specs = (
        P("tm", None, "space", None),
        P("tm", None, "space", None),
        P("tm", None, "space", None),
    )
    return jax.shard_map(body, mesh=mesh, in_specs=in_specs, out_specs=out_specs, check_vma=False)
```

```python
import functools

import jax
import jax.numpy as jnp
from jax import lax
from jax.experimental import pallas as pl
from jax.experimental.pallas import tpu as pltpu
from jax.sharding import PartitionSpec as P

FINE_STEPS = 8
LORENTZ = 0.3
FRICTION = 0.01
TIME_STEP = 0.28
ROWS = 8
LANES = 128
GROUP = 16

ALPHA = 0.6265382932707997
QUAD_A = 0.3734617067292003
QUAD_B = 0.2660119396638869

VMEM = pl.BlockSpec(memory_space=pltpu.VMEM)
SMEM = pl.BlockSpec(memory_space=pltpu.SMEM)


def iotas():
    sub = lax.broadcasted_iota(jnp.int32, (ROWS, LANES), 0)
    lane = lax.broadcasted_iota(jnp.int32, (ROWS, LANES), 1)
    return sub, lane


def strip(k):
    start = LANES + k * LANES
    return pl.ds(start if isinstance(start, int) else pl.multiple_of(start, LANES), LANES)


def guards(buf, tiles, shift, strips):
    _, lane = iotas()
    even = lane % 2 == 0
    for t in tiles:
        for comp, sign in ((0, 1.0), (2, -1.0)):
            first = buf[t, comp, :, strip(0)]
            last = buf[t, comp, :, strip(strips - 1)]
            low = sign * pltpu.roll(first, LANES - shift, 1)
            high = sign * pltpu.roll(last, shift, 1)
            if shift == 2:
                low = jnp.where(even, low, pltpu.roll(last, 1, 1))
                high = jnp.where(even, pltpu.roll(first, LANES - 1, 1), high)
            buf[t, comp, :, strip(-1)] = low
            buf[t, comp, :, strip(strips)] = high


def stage(dst, src, base, weight, length, field, tiles, shift, cell, strips, group):
    factor = length / (2.0 * cell)
    drag = FRICTION * length
    sub, lane = iotas()
    rows_high = sub >= ROWS - shift
    rows_low = sub < shift
    lanes_high = lane >= LANES - shift
    lanes_low = lane < shift
    slots = dst.shape[0]
    group = min(group, strips)

    def block(g, carry):
        for j in range(group):
            k = g * group + j
            here = strip(k)
            cache = {}

            def get(comp, t):
                t = min(max(t, 0), slots - 1)
                if (comp, t) not in cache:
                    cache[comp, t] = src[t, comp, :, here]
                return cache[comp, t]

            for t in tiles:
                height, east, north = get(0, t), get(1, t), get(2, t)

                def row_diff(comp, centre):
                    before = jnp.where(rows_high, get(comp, t - 1), centre)
                    after = jnp.where(rows_low, get(comp, t + 1), centre)
                    return pltpu.roll(after, ROWS - shift, 0) - pltpu.roll(before, shift, 0)

                def col_diff(comp, centre):
                    before = jnp.where(lanes_high, src[t, comp, :, strip(k - 1)], centre)
                    after = jnp.where(lanes_low, src[t, comp, :, strip(k + 1)], centre)
                    return pltpu.roll(after, LANES - shift, 1) - pltpu.roll(before, shift, 1)

                b = field[t, :, pl.ds(here.start - LANES, LANES)]
                dx, dy = row_diff(0, height), col_diff(0, height)
                rise = row_diff(1, east) + col_diff(2, north)
                if base is src:
                    new_height = weight * height - factor * rise
                    new_east = (weight - drag) * east + factor * (b * dy - dx)
                    new_north = (weight - drag) * north - factor * (b * dx + dy)
                else:
                    old = [base[t, comp, :, here] for comp in range(3)]
                    if weight != 1.0:
                        old = [weight * o for o in old]
                    new_height = old[0] - factor * rise
                    new_east = old[1] - drag * east + factor * (b * dy - dx)
                    new_north = old[2] - drag * north - factor * (b * dx + dy)
                dst[t, 0, :, here] = new_height
                dst[t, 1, :, here] = new_east
                dst[t, 2, :, here] = new_north
        return carry

    lax.fori_loop(0, strips // group, block, 0)
    guards(dst, tiles, shift, strips)


def pair_mean(x, sub, lane):
    x = x + jnp.where(sub % 2 == 0, pltpu.roll(x, ROWS - 1, 0), pltpu.roll(x, 1, 0))
    x = x + jnp.where(lane % 2 == 0, pltpu.roll(x, LANES - 1, 1), pltpu.roll(x, 1, 1))
    return 0.25 * x


def flip_tiles(position, count, halo, first, copy_row):
    low = jnp.maximum(halo - position, 0)
    high = jnp.maximum(position + halo - (count - 1), 0)

    def fill_low(q, carry):
        for r in range(ROWS):
            copy_row(first + halo - position - 1 - q, ROWS - 1 - r, first + halo - position + q, r)
        return carry

    def fill_high(q, carry):
        for r in range(ROWS):
            copy_row(
                first + count + q - position + halo,
                ROWS - 1 - r,
                first + count - 1 - q - position + halo,
                r,
            )
        return carry

    lax.fori_loop(0, low, fill_low, 0)
    lax.fori_loop(0, high, fill_high, 0)


def flip_state(buf, position, count, halo, first=0):
    cols = pl.ds(LANES, buf.shape[3] - 2 * LANES)

    def copy_row(t_to, r_to, t_from, r_from):
        for comp, sign in ((0, 1.0), (1, -1.0), (2, 1.0)):
            buf[t_to, comp, pl.ds(r_to, 1), cols] = sign * buf[t_from, comp, pl.ds(r_from, 1), cols]

    flip_tiles(position, count, halo, first, copy_row)


def flip_field(field, position, count, halo):
    def copy_row(t_to, r_to, t_from, r_from):
        field[t_to, pl.ds(r_to, 1), :] = -field[t_from, pl.ds(r_from, 1), :]

    flip_tiles(position, count, halo, 0, copy_row)


def folded(left, right, lane):
    return jnp.where(lane % 2 == 0, left, right)


def unfolded(x, lane):
    left = jnp.where(lane % 2 == 0, x, pltpu.roll(x, 1, 1))
    right = jnp.where(lane % 2 == 1, x, pltpu.roll(x, LANES - 1, 1))
    return left, right


def zipped(even, odd, sub):
    return jnp.where(sub % 2 == 0, even, odd)


def unzipped(x, sub):
    even = jnp.where(sub % 2 == 0, x, pltpu.roll(x, 1, 0))
    odd = jnp.where(sub % 2 == 1, x, pltpu.roll(x, ROWS - 1, 0))
    return even, odd


def places(position):
    core = lax.rem(position, 2)
    chip = lax.div(position, 2)
    side = 1 - 2 * core
    near = 2 * (2 * lax.rem(chip, 2) - 1)
    far = 4 * (2 * lax.rem(lax.div(chip, 2), 2) - 1)
    return side, near, far


def fine_kernel(
    count, strips, pos, state, field, near_a, near_b, third, sib, sib_a, sib_b, coarse,
    out, detail, message, one, two, window,
):
    position = pos[0]
    side, near, _ = places(position)
    cols = pl.ds(LANES, strips * LANES)
    arrived = (
        (near_a, near), (near_b, -near), (third, -3 * side),
        (sib, side), (sib_a, near + side), (sib_b, side - near),
    )
    window[3] = LORENTZ * field[...]
    for comp in range(3):
        one[3, comp, :, cols] = state[comp]
    for ref, offset in arrived:
        slot = 3 + offset
        window[slot] = LORENTZ * ref[3]
        for comp in range(3):
            one[slot, comp, :, cols] = ref[comp]
    flip_field(window, position, count, 3)
    flip_state(one, position, count, 3)
    guards(one, range(7), 1, strips)

    run = functools.partial(stage, field=window, shift=1, cell=1.0, strips=strips, group=GROUP)
    a, b = one, two
    for reach, quads, lines in ((3, 3, 2), (2, 3, 2), (1, 2, 4)):
        tiles = range(3 - reach, 4 + reach)

        def quad(step, carry, a=a, b=b, tiles=tiles):
            run(b, a, a, QUAD_A, QUAD_B * TIME_STEP, tiles=tiles)
            run(a, b, a, 1.0, TIME_STEP, tiles=tiles)
            return carry

        lax.fori_loop(0, quads, quad, 0)
        for n in range(lines):
            if n == lines - 1:
                tiles = range(4 - reach, 3 + reach)
            run(b, a, a, 1.0, ALPHA * TIME_STEP, tiles=tiles)
            a, b = b, a

    sub, lane = iotas()
    keep = jnp.where(pos[1] == 0, 0.0, 1.0)
    half = strips // 2
    for k in range(half):
        means = []
        for comp in range(3):
            sides = []
            both = unfolded(coarse[comp, :, pl.ds(k * LANES, LANES)], lane)
            for s, less in zip((k, k + half), both):
                lanes = pl.ds(s * LANES, LANES)
                value = a[3, comp, :, strip(s)]
                out[comp, :, lanes] = value
                rest = value - keep * less
                detail[comp, :, lanes] = rest
                sides.append(pair_mean(rest, sub, lane))
            means.append(folded(*sides, lane))
        sides = [pair_mean(field[:, pl.ds(s * LANES, LANES)], sub, lane) for s in (k, k + half)]
        lanes = pl.ds(k * LANES, LANES)
        message[0, :, lanes] = zipped(means[0], means[1], sub)
        message[1, :, lanes] = zipped(means[2], LORENTZ * folded(*sides, lane), sub)


def coarse_step(bufs, field, tiles_of, strips, group):
    one, two, three = bufs
    length = FINE_STEPS * TIME_STEP
    run = functools.partial(stage, base=one, field=field, shift=2, cell=2.0, strips=strips, group=group)
    run(two, one, weight=1.0, length=length / 3.0, tiles=tiles_of(0))
    run(three, two, weight=1.0, length=length / 2.0, tiles=tiles_of(1))
    run(one, three, weight=1.0, length=length, tiles=tiles_of(2))


def coarse_kernel(
    count, strips, pos, state, field, sib, sib_a, sib_b, out, short, one, two, three, window
):
    position = pos[0]
    side, near, _ = places(position)
    sub, lane = iotas()
    half = strips // 2

    def put(slot, ref, plane):
        for k in range(half):
            pairs = [pl.ds(s * LANES, LANES) for s in (k, k + half)]
            for comp in range(3):
                means = [pair_mean(ref[comp, :, lanes], sub, lane) for lanes in pairs]
                one[slot, comp, :, strip(k)] = folded(*means, lane)
            means = [pair_mean(plane[:, lanes], sub, lane) for lanes in pairs]
            window[slot, :, pl.ds(k * LANES, LANES)] = LORENTZ * folded(*means, lane)

    put(1, state, field)
    put(1 + side, sib, sib.at[3])
    for ref, sign in ((sib_a, 1), (sib_b, -1)):

        @pl.when(sign * near + side == -side)
        def _(ref=ref):
            put(1 - side, ref, ref.at[3])

    flip_field(window, position, count, 1)
    flip_state(one, position, count, 1)
    guards(one, range(3), 2, half)
    coarse_step((one, two, three), window, lambda n: range(3) if n < 2 else (1,), half, GROUP)
    for k in range(half):
        for comp in range(3):
            value = one[1, comp, :, strip(k)]
            short[comp, :, pl.ds(k * LANES, LANES)] = value
            for s, part in zip((k, k + half), unfolded(value, lane)):
                out[comp, :, pl.ds(s * LANES, LANES)] = part


def powers_kernel(
    count, strips, pos, own, sib, near_a, near_b, far_a, far_b, fifth, others, *refs
):
    outs, (one, two, three, window) = refs[:3], refs[3:]
    position = pos[0]
    side, near, far = places(position)
    sub, lane = iotas()
    half = strips // 2
    arrived = (
        (own, 0, 0), (sib, 0, side), (near_a, 0, near), (near_b, 0, -near), (far_a, 0, far),
        (far_b, 0, -far), (fifth, 0, -5 * side), (others, 0, near + side),
        (others, 2, side - near), (others, 4, far + side), (others, 6, side - far),
    )
    for ref, at, offset in arrived:
        slot = 5 + offset
        for k in range(half):
            lanes = pl.ds(k * LANES, LANES)
            height, east = unzipped(ref[at, :, lanes], sub)
            north, plane = unzipped(ref[at + 1, :, lanes], sub)
            one[slot, 0, :, strip(k)] = height
            one[slot, 1, :, strip(k)] = east
            one[slot, 2, :, strip(k)] = north
            window[slot, :, lanes] = plane
    flip_field(window, position, count, 5)
    flip_state(one, position, count, 5)
    guards(one, range(11), 2, half)
    for s in range(6):

        def tiles_of(n, s=s):
            reach = -(-2 * (18 - 3 * s - n - 1) // ROWS)
            return range(5 - reach, 6 + reach)

        coarse_step((one, two, three), window, tiles_of, half, 8)
        out = outs[s // 2]
        for k in range(half):
            lanes = pl.ds(k * LANES, LANES)
            height, east, north = [one[5, comp, :, strip(k)] for comp in range(3)]
            out[s % 2, :, lanes] = zipped(height, east, sub)
            if s % 2 == 0:
                out[2, :, lanes] = north
            else:
                out[2, :, lanes] = zipped(out[2, :, lanes], north, sub)


def final_kernel(strips, pos, own, other, detail, anchor, out):
    sub, lane = iotas()
    half = strips // 2
    first = pos[1] == 0
    for k in range(half):
        lanes = pl.ds(k * LANES, LANES)
        height, east = unzipped(own[0, :, lanes] + other[0, :, lanes], sub)
        north = unzipped(own[2, :, lanes], sub)[0] + unzipped(other[1, :, lanes], sub)[1]
        for comp, value in enumerate((height, east, north)):
            for s, part in zip((k, k + half), unfolded(value, lane)):
                wide = pl.ds(s * LANES, LANES)
                total = part + detail[comp, :, wide]
                out[comp, :, wide] = jnp.where(first, anchor[comp, :, wide], total)


def call(kernel, outs, buffers, name, *args):
    return pl.pallas_call(
        kernel,
        out_shape=outs,
        in_specs=[SMEM] + [VMEM] * (len(args) - 1),
        out_specs=[VMEM] * len(outs),
        scratch_shapes=buffers,
        compiler_params=pltpu.CompilerParams(vmem_limit_bytes=48 * 1024 * 1024),
        name=name,
    )(*args)


def swap(block, partner):
    slices, count = lax.axis_size("tm"), lax.axis_size("space")
    pairs = [(i, partner(i)) for i in range(count)]
    pairs = [(i, j) for i, j in pairs if 0 <= j < count]
    return lax.ppermute(block, "space", pairs)


def later(block, distance):
    slices = lax.axis_size("tm")
    return lax.ppermute(block, "tm", [(m, m + distance) for m in range(slices - distance)])


def two_legs():
    slices, count = lax.axis_size("tm"), lax.axis_size("space")
    run = min(8, count // 2)
    legs = [], []
    for m in range(slices - 1):
        for i in range(count):
            y, upper = divmod(m, 2)
            group, low = divmod(i // 2, run)
            way = 1 if i % 2 == 0 else -1
            upper, low = divmod((upper * run + low + way * (run // 2)) % (2 * run), run)
            stop = (2 * y + upper) * count + 2 * (group * run + low) + i % 2
            legs[0].append((m * count + i, stop))
            legs[1].append((stop, (m + 1) * count + i))
    return legs


def sibling(i):
    return i + 1 - 2 * (i % 2)


def near_odd(i):
    return i + (2 if (i // 2) % 2 == 1 else -2)


def near_even(i):
    return i - (2 if (i // 2) % 2 == 1 else -2)


def far_odd(i):
    return i + (4 if (i // 4) % 2 == 1 else -4)


def far_even(i):
    return i - (4 if (i // 4) % 2 == 1 else -4)


def third(i):
    return i - 3 if i % 2 == 0 else i + 3


def fifth(i):
    return i - 5 if i % 2 == 0 else i + 5


def body(start_state, vertical_field):
    state = start_state[0]
    cols = state.shape[2]
    strips = cols // LANES
    count = lax.axis_size("space")
    pos = jnp.stack([lax.axis_index("space"), lax.axis_index("tm")]).astype(jnp.int32)
    shape = lambda *dims: jax.ShapeDtypeStruct(dims, jnp.float32)
    tile = shape(3, ROWS, cols)
    buf = lambda tiles, wide: pltpu.VMEM((tiles, 3, ROWS, wide + 2 * LANES), jnp.float32)
    plane = lambda tiles, wide: pltpu.VMEM((tiles, ROWS, wide), jnp.float32)

    sent = jnp.concatenate([state, vertical_field[None]], axis=0)
    sib = swap(sent, sibling)
    b = swap(sent, near_even)
    q = swap(sent, third)
    a = swap(sent, near_odd)
    a, b, q = lax.optimization_barrier((a, b, q))
    sib_b, sib_a = swap(b, sibling), swap(a, sibling)
    coarse_end, short = call(
        functools.partial(coarse_kernel, count, strips),
        [tile, shape(3, ROWS, cols // 2)],
        [buf(3, cols // 2)] * 3 + [plane(3, cols // 2)],
        "coarse",
        pos, state, vertical_field, sib, sib_a, sib_b,
    )
    fine_end, detail, message = call(
        functools.partial(fine_kernel, count, strips),
        [tile, tile, shape(2, ROWS, cols // 2)],
        [buf(7, cols), buf(7, cols), plane(7, cols)],
        "fine",
        pos, state, vertical_field, a, b, q, sib, sib_a, sib_b, short,
    )
    legs = two_legs()
    halfway = lax.ppermute(detail, ("tm", "space"), legs[0])
    sib = swap(message, sibling)
    b = swap(message, near_even)
    d = swap(message, far_even)
    q = swap(message, fifth)
    c = swap(message, far_odd)
    a = swap(message, near_odd)
    a, b, c, d, q, sib, halfway = lax.optimization_barrier((a, b, c, d, q, sib, halfway))
    arrived = lax.ppermute(halfway, ("tm", "space"), legs[1])
    others = swap(jnp.concatenate([a, b, c, d], axis=0), sibling)
    powers = call(
        functools.partial(powers_kernel, count, strips),
        [shape(3, ROWS, cols // 2)] * 3,
        [buf(11, cols // 2)] * 3 + [plane(11, cols // 2)],
        "powers",
        pos, message, sib, a, b, c, d, q, others,
    )
    powers, arrived = lax.optimization_barrier((powers, arrived))
    own = sum(later(x, 2 * d + 2) for d, x in enumerate(powers))
    other = later(own[1:], 1)
    (new_start,) = call(
        functools.partial(final_kernel, strips),
        [tile],
        [],
        "final",
        pos, own, other, arrived, state,
    )
    return (new_start[None], fine_end[None], coarse_end[None])


def solution(mesh):
    in_specs = (P("tm", None, "space", None), P("space", None))
    out_specs = (
        P("tm", None, "space", None),
        P("tm", None, "space", None),
        P("tm", None, "space", None),
    )
    return jax.shard_map(body, mesh=mesh, in_specs=in_specs, out_specs=out_specs, check_vma=False)
```

```python
import functools

import jax
import jax.numpy as jnp
from jax import lax
from jax.experimental import pallas as pl
from jax.experimental.pallas import tpu as pltpu
from jax.sharding import PartitionSpec as P

FINE_STEPS = 8
LORENTZ = 0.3
FRICTION = 0.01
TIME_STEP = 0.28
ROWS = 8
LANES = 128

ALPHA = 0.6265382932707997
QUAD_A = 0.3734617067292003
QUAD_B = 0.2660119396638869

VMEM = pl.BlockSpec(memory_space=pltpu.VMEM)
SMEM = pl.BlockSpec(memory_space=pltpu.SMEM)


def iotas():
    sub = lax.broadcasted_iota(jnp.int32, (ROWS, LANES), 0)
    lane = lax.broadcasted_iota(jnp.int32, (ROWS, LANES), 1)
    return sub, lane


def strip(k):
    start = LANES + k * LANES
    return pl.ds(start if isinstance(start, int) else pl.multiple_of(start, LANES), LANES)


def guard_pair(sign, first, last, shift, even):
    low = sign * pltpu.roll(first, LANES - shift, 1)
    high = sign * pltpu.roll(last, shift, 1)
    if shift == 2:
        low = jnp.where(even, low, pltpu.roll(last, 1, 1))
        high = jnp.where(even, pltpu.roll(first, LANES - 1, 1), high)
    return low, high


def guards(buf, tiles, shift, strips):
    _, lane = iotas()
    even = lane % 2 == 0
    for t in tiles:
        for comp, sign in ((0, 1.0), (2, -1.0)):
            first = buf[t, comp, :, strip(0)]
            last = buf[t, comp, :, strip(strips - 1)]
            low, high = guard_pair(sign, first, last, shift, even)
            buf[t, comp, :, strip(-1)] = low
            buf[t, comp, :, strip(strips)] = high


def stage(dst, src, base, weight, length, field, tiles, shift, cell, strips):
    factor = length / (2.0 * cell)
    drag = FRICTION * length
    sub, lane = iotas()
    rows_high = sub >= ROWS - shift
    rows_low = sub < shift
    lanes_high = lane >= LANES - shift
    lanes_low = lane < shift
    slots = dst.shape[0]
    even = lane % 2 == 0
    firsts = {}
    for k in range(strips):
        here = strip(k)
        cache = {}

        def get(comp, t):
            t = min(max(t, 0), slots - 1)
            if (comp, t) not in cache:
                cache[comp, t] = src[t, comp, :, here]
            return cache[comp, t]

        for t in tiles:
            height, east, north = get(0, t), get(1, t), get(2, t)

            def row_diff(comp, centre):
                before = jnp.where(rows_high, get(comp, t - 1), centre)
                after = jnp.where(rows_low, get(comp, t + 1), centre)
                return pltpu.roll(after, ROWS - shift, 0) - pltpu.roll(before, shift, 0)

            def col_diff(comp, centre):
                before = jnp.where(lanes_high, src[t, comp, :, strip(k - 1)], centre)
                after = jnp.where(lanes_low, src[t, comp, :, strip(k + 1)], centre)
                return pltpu.roll(after, LANES - shift, 1) - pltpu.roll(before, shift, 1)

            b = field[t, :, pl.ds(here.start - LANES, LANES)]
            dx, dy = row_diff(0, height), col_diff(0, height)
            rise = row_diff(1, east) + col_diff(2, north)
            if base is src:
                new_height = weight * height - factor * rise
                new_east = (weight - drag) * east + factor * (b * dy - dx)
                new_north = (weight - drag) * north - factor * (b * dx + dy)
            else:
                old = [base[t, comp, :, here] for comp in range(3)]
                if weight != 1.0:
                    old = [weight * o for o in old]
                new_height = old[0] - factor * rise
                new_east = old[1] - drag * east + factor * (b * dy - dx)
                new_north = old[2] - drag * north - factor * (b * dx + dy)
            dst[t, 0, :, here] = new_height
            dst[t, 1, :, here] = new_east
            dst[t, 2, :, here] = new_north
            if k == 0:
                firsts[t] = new_height, new_north
            if k == strips - 1:
                for comp, sign, first, final in zip(
                    (0, 2), (1.0, -1.0), firsts[t], (new_height, new_north)
                ):
                    low, high = guard_pair(sign, first, final, shift, even)
                    dst[t, comp, :, strip(-1)] = low
                    dst[t, comp, :, strip(strips)] = high


def pair_mean(x, sub, lane):
    x = x + jnp.where(sub % 2 == 0, pltpu.roll(x, ROWS - 1, 0), pltpu.roll(x, 1, 0))
    x = x + jnp.where(lane % 2 == 0, pltpu.roll(x, LANES - 1, 1), pltpu.roll(x, 1, 1))
    return 0.25 * x


def flip_tiles(position, count, halo, first, copy_row):
    low = jnp.maximum(halo - position, 0)
    high = jnp.maximum(position + halo - (count - 1), 0)

    def fill_low(q, carry):
        for r in range(ROWS):
            copy_row(first + halo - position - 1 - q, ROWS - 1 - r, first + halo - position + q, r)
        return carry

    def fill_high(q, carry):
        for r in range(ROWS):
            copy_row(
                first + count + q - position + halo,
                ROWS - 1 - r,
                first + count - 1 - q - position + halo,
                r,
            )
        return carry

    lax.fori_loop(0, low, fill_low, 0)
    lax.fori_loop(0, high, fill_high, 0)


def flip_state(buf, position, count, halo, first=0):
    cols = pl.ds(LANES, buf.shape[3] - 2 * LANES)

    def copy_row(t_to, r_to, t_from, r_from):
        for comp, sign in ((0, 1.0), (1, -1.0), (2, 1.0)):
            buf[t_to, comp, pl.ds(r_to, 1), cols] = sign * buf[t_from, comp, pl.ds(r_from, 1), cols]

    flip_tiles(position, count, halo, first, copy_row)


def flip_field(field, position, count, halo):
    def copy_row(t_to, r_to, t_from, r_from):
        field[t_to, pl.ds(r_to, 1), :] = -field[t_from, pl.ds(r_from, 1), :]

    flip_tiles(position, count, halo, 0, copy_row)


def folded(left, right, lane):
    return jnp.where(lane % 2 == 0, left, right)


def unfolded(x, lane):
    left = jnp.where(lane % 2 == 0, x, pltpu.roll(x, 1, 1))
    right = jnp.where(lane % 2 == 1, x, pltpu.roll(x, LANES - 1, 1))
    return left, right


def zipped(even, odd, sub):
    return jnp.where(sub % 2 == 0, even, odd)


def unzipped(x, sub):
    even = jnp.where(sub % 2 == 0, x, pltpu.roll(x, 1, 0))
    odd = jnp.where(sub % 2 == 1, x, pltpu.roll(x, ROWS - 1, 0))
    return even, odd


def places(position):
    core = lax.rem(position, 2)
    chip = lax.div(position, 2)
    side = 1 - 2 * core
    near = 2 * (2 * lax.rem(chip, 2) - 1)
    far = 4 * (2 * lax.rem(lax.div(chip, 2), 2) - 1)
    return side, near, far


def fine_kernel(
    count, strips, pos, state, field, near_a, near_b, third, sib, sib_a, sib_b, coarse,
    out, detail, message, one, two, window,
):
    position = pos[0]
    side, near, _ = places(position)
    cols = pl.ds(LANES, strips * LANES)
    arrived = (
        (near_a, near), (near_b, -near), (third, -3 * side),
        (sib, side), (sib_a, near + side), (sib_b, side - near),
    )
    window[3] = LORENTZ * field[...]
    for comp in range(3):
        one[3, comp, :, cols] = state[comp]
    for ref, offset in arrived:
        slot = 3 + offset
        window[slot] = LORENTZ * ref[3]
        for comp in range(3):
            one[slot, comp, :, cols] = ref[comp]
    flip_field(window, position, count, 3)
    flip_state(one, position, count, 3)
    guards(one, range(7), 1, strips)

    run = functools.partial(stage, field=window, shift=1, cell=1.0, strips=strips)
    a, b = one, two
    for reach, quads, lines in ((3, 3, 2), (2, 3, 2), (1, 2, 4)):
        tiles = range(3 - reach, 4 + reach)

        def quad(step, carry, a=a, b=b, tiles=tiles):
            run(b, a, a, QUAD_A, QUAD_B * TIME_STEP, tiles=tiles)
            run(a, b, a, 1.0, TIME_STEP, tiles=tiles)
            return carry

        lax.fori_loop(0, quads, quad, 0)
        for n in range(lines):
            if n == lines - 1:
                tiles = range(4 - reach, 3 + reach)
            run(b, a, a, 1.0, ALPHA * TIME_STEP, tiles=tiles)
            a, b = b, a

    sub, lane = iotas()
    keep = jnp.where(pos[1] == 0, 0.0, 1.0)
    half = strips // 2
    for k in range(half):
        means = []
        for comp in range(3):
            sides = []
            both = unfolded(coarse[comp, :, pl.ds(k * LANES, LANES)], lane)
            for s, less in zip((k, k + half), both):
                lanes = pl.ds(s * LANES, LANES)
                value = a[3, comp, :, strip(s)]
                out[comp, :, lanes] = value
                rest = value - keep * less
                detail[comp, :, lanes] = rest
                sides.append(pair_mean(rest, sub, lane))
            means.append(folded(*sides, lane))
        sides = [pair_mean(field[:, pl.ds(s * LANES, LANES)], sub, lane) for s in (k, k + half)]
        lanes = pl.ds(k * LANES, LANES)
        message[0, :, lanes] = zipped(means[0], means[1], sub)
        message[1, :, lanes] = zipped(means[2], LORENTZ * folded(*sides, lane), sub)


def coarse_step(bufs, field, tiles_of, strips):
    one, two, three = bufs
    length = FINE_STEPS * TIME_STEP
    run = functools.partial(stage, base=one, field=field, shift=2, cell=2.0, strips=strips)
    run(two, one, weight=1.0, length=length / 3.0, tiles=tiles_of(0))
    run(three, two, weight=1.0, length=length / 2.0, tiles=tiles_of(1))
    run(one, three, weight=1.0, length=length, tiles=tiles_of(2))


def coarse_kernel(
    count, strips, pos, state, field, sib, sib_a, sib_b, out, short, one, two, three, window
):
    position = pos[0]
    side, near, _ = places(position)
    sub, lane = iotas()
    half = strips // 2

    def put(slot, ref, plane):
        for k in range(half):
            pairs = [pl.ds(s * LANES, LANES) for s in (k, k + half)]
            for comp in range(3):
                means = [pair_mean(ref[comp, :, lanes], sub, lane) for lanes in pairs]
                one[slot, comp, :, strip(k)] = folded(*means, lane)
            means = [pair_mean(plane[:, lanes], sub, lane) for lanes in pairs]
            window[slot, :, pl.ds(k * LANES, LANES)] = LORENTZ * folded(*means, lane)

    put(1, state, field)
    put(1 + side, sib, sib.at[3])
    for ref, sign in ((sib_a, 1), (sib_b, -1)):

        @pl.when(sign * near + side == -side)
        def _(ref=ref):
            put(1 - side, ref, ref.at[3])

    flip_field(window, position, count, 1)
    flip_state(one, position, count, 1)
    guards(one, range(3), 2, half)
    coarse_step((one, two, three), window, lambda n: range(3) if n < 2 else (1,), half)
    for k in range(half):
        for comp in range(3):
            value = one[1, comp, :, strip(k)]
            short[comp, :, pl.ds(k * LANES, LANES)] = value
            for s, part in zip((k, k + half), unfolded(value, lane)):
                out[comp, :, pl.ds(s * LANES, LANES)] = part


def powers_kernel(
    count, strips, pos, own, sib, near_a, near_b, far_a, far_b, fifth, others, *refs
):
    outs, (one, two, three, window) = refs[:3], refs[3:]
    position = pos[0]
    side, near, far = places(position)
    sub, lane = iotas()
    half = strips // 2
    arrived = (
        (own, 0, 0), (sib, 0, side), (near_a, 0, near), (near_b, 0, -near), (far_a, 0, far),
        (far_b, 0, -far), (fifth, 0, -5 * side), (others, 0, near + side),
        (others, 2, side - near), (others, 4, far + side), (others, 6, side - far),
    )
    for ref, at, offset in arrived:
        slot = 5 + offset
        for k in range(half):
            lanes = pl.ds(k * LANES, LANES)
            height, east = unzipped(ref[at, :, lanes], sub)
            north, plane = unzipped(ref[at + 1, :, lanes], sub)
            one[slot, 0, :, strip(k)] = height
            one[slot, 1, :, strip(k)] = east
            one[slot, 2, :, strip(k)] = north
            window[slot, :, lanes] = plane
    flip_field(window, position, count, 5)
    flip_state(one, position, count, 5)
    guards(one, range(11), 2, half)
    for s in range(6):

        def tiles_of(n, s=s):
            reach = -(-2 * (18 - 3 * s - n - 1) // ROWS)
            return range(5 - reach, 6 + reach)

        coarse_step((one, two, three), window, tiles_of, half)
        out = outs[s // 2]
        for k in range(half):
            lanes = pl.ds(k * LANES, LANES)
            height, east, north = [one[5, comp, :, strip(k)] for comp in range(3)]
            out[s % 2, :, lanes] = zipped(height, east, sub)
            if s % 2 == 0:
                out[2, :, lanes] = north
            else:
                out[2, :, lanes] = zipped(out[2, :, lanes], north, sub)


def final_kernel(strips, pos, own, other, detail, anchor, out):
    sub, lane = iotas()
    half = strips // 2
    first = pos[1] == 0
    for k in range(half):
        lanes = pl.ds(k * LANES, LANES)
        height, east = unzipped(own[0, :, lanes] + other[0, :, lanes], sub)
        north = unzipped(own[2, :, lanes], sub)[0] + unzipped(other[1, :, lanes], sub)[1]
        for comp, value in enumerate((height, east, north)):
            for s, part in zip((k, k + half), unfolded(value, lane)):
                wide = pl.ds(s * LANES, LANES)
                total = part + detail[comp, :, wide]
                out[comp, :, wide] = jnp.where(first, anchor[comp, :, wide], total)


def call(kernel, outs, buffers, name, *args):
    return pl.pallas_call(
        kernel,
        out_shape=outs,
        in_specs=[SMEM] + [VMEM] * (len(args) - 1),
        out_specs=[VMEM] * len(outs),
        scratch_shapes=buffers,
        compiler_params=pltpu.CompilerParams(vmem_limit_bytes=48 * 1024 * 1024),
        name=name,
    )(*args)


def swap(block, partner):
    slices, count = lax.axis_size("tm"), lax.axis_size("space")
    pairs = [(i, partner(i)) for i in range(count)]
    pairs = [(i, j) for i, j in pairs if 0 <= j < count]
    return lax.ppermute(block, "space", pairs)


def later(block, distance):
    slices = lax.axis_size("tm")
    return lax.ppermute(block, "tm", [(m, m + distance) for m in range(slices - distance)])


def two_legs():
    slices, count = lax.axis_size("tm"), lax.axis_size("space")
    run = min(8, count // 2)
    legs = [], []
    for m in range(slices - 1):
        for i in range(count):
            y, upper = divmod(m, 2)
            group, low = divmod(i // 2, run)
            way = 1 if i % 2 == 0 else -1
            upper, low = divmod((upper * run + low + way * (run // 2)) % (2 * run), run)
            stop = (2 * y + upper) * count + 2 * (group * run + low) + i % 2
            legs[0].append((m * count + i, stop))
            legs[1].append((stop, (m + 1) * count + i))
    return legs


def sibling(i):
    return i + 1 - 2 * (i % 2)


def near_odd(i):
    return i + (2 if (i // 2) % 2 == 1 else -2)


def near_even(i):
    return i - (2 if (i // 2) % 2 == 1 else -2)


def far_odd(i):
    return i + (4 if (i // 4) % 2 == 1 else -4)


def far_even(i):
    return i - (4 if (i // 4) % 2 == 1 else -4)


def third(i):
    return i - 3 if i % 2 == 0 else i + 3


def fifth(i):
    return i - 5 if i % 2 == 0 else i + 5


def body(start_state, vertical_field):
    state = start_state[0]
    cols = state.shape[2]
    strips = cols // LANES
    count = lax.axis_size("space")
    pos = jnp.stack([lax.axis_index("space"), lax.axis_index("tm")]).astype(jnp.int32)
    shape = lambda *dims: jax.ShapeDtypeStruct(dims, jnp.float32)
    tile = shape(3, ROWS, cols)
    buf = lambda tiles, wide: pltpu.VMEM((tiles, 3, ROWS, wide + 2 * LANES), jnp.float32)
    plane = lambda tiles, wide: pltpu.VMEM((tiles, ROWS, wide), jnp.float32)

    sent = jnp.concatenate([state, vertical_field[None]], axis=0)
    sib = swap(sent, sibling)
    b = swap(sent, near_even)
    q = swap(sent, third)
    a = swap(sent, near_odd)
    a, b, q = lax.optimization_barrier((a, b, q))
    sib_b, sib_a = swap(b, sibling), swap(a, sibling)
    coarse_end, short = call(
        functools.partial(coarse_kernel, count, strips),
        [tile, shape(3, ROWS, cols // 2)],
        [buf(3, cols // 2)] * 3 + [plane(3, cols // 2)],
        "coarse",
        pos, state, vertical_field, sib, sib_a, sib_b,
    )
    fine_end, detail, message = call(
        functools.partial(fine_kernel, count, strips),
        [tile, tile, shape(2, ROWS, cols // 2)],
        [buf(7, cols), buf(7, cols), plane(7, cols)],
        "fine",
        pos, state, vertical_field, a, b, q, sib, sib_a, sib_b, short,
    )
    legs = two_legs()
    halfway = lax.ppermute(detail, ("tm", "space"), legs[0])
    sib = swap(message, sibling)
    b = swap(message, near_even)
    d = swap(message, far_even)
    q = swap(message, fifth)
    c = swap(message, far_odd)
    a = swap(message, near_odd)
    a, b, c, d, q, sib = lax.optimization_barrier((a, b, c, d, q, sib))
    others = swap(jnp.concatenate([a, b, c, d], axis=0), sibling)
    powers = call(
        functools.partial(powers_kernel, count, strips),
        [shape(3, ROWS, cols // 2)] * 3,
        [buf(11, cols // 2)] * 3 + [plane(11, cols // 2)],
        "powers",
        pos, message, sib, a, b, c, d, q, others,
    )
    own = sum(later(x, 2 * d + 2) for d, x in enumerate(powers))
    arrived = lax.ppermute(halfway, ("tm", "space"), legs[1])
    other = later(own[1:], 1)
    (new_start,) = call(
        functools.partial(final_kernel, strips),
        [tile],
        [],
        "final",
        pos, own, other, arrived, state,
    )
    return (new_start[None], fine_end[None], coarse_end[None])


def solution(mesh):
    in_specs = (P("tm", None, "space", None), P("space", None))
    out_specs = (
        P("tm", None, "space", None),
        P("tm", None, "space", None),
        P("tm", None, "space", None),
    )
    return jax.shard_map(body, mesh=mesh, in_specs=in_specs, out_specs=out_specs, check_vma=False)
```

```python
import functools

import jax
import jax.numpy as jnp
from jax import lax
from jax.experimental import pallas as pl
from jax.experimental.pallas import tpu as pltpu
from jax.sharding import PartitionSpec as P

FINE_STEPS = 8
LORENTZ = 0.3
FRICTION = 0.01
TIME_STEP = 0.28
ROWS = 8
LANES = 128
GROUP = 16

ALPHA = 0.6265382932707997
QUAD_A = 0.3734617067292003
QUAD_B = 0.2660119396638869

VMEM = pl.BlockSpec(memory_space=pltpu.VMEM)
SMEM = pl.BlockSpec(memory_space=pltpu.SMEM)


def iotas():
    sub = lax.broadcasted_iota(jnp.int32, (ROWS, LANES), 0)
    lane = lax.broadcasted_iota(jnp.int32, (ROWS, LANES), 1)
    return sub, lane


def strip(k):
    start = LANES + k * LANES
    return pl.ds(start if isinstance(start, int) else pl.multiple_of(start, LANES), LANES)


def guards(buf, tiles, shift, strips):
    _, lane = iotas()
    even = lane % 2 == 0
    for t in tiles:
        for comp, sign in ((0, 1.0), (2, -1.0)):
            first = buf[t, comp, :, strip(0)]
            last = buf[t, comp, :, strip(strips - 1)]
            low = sign * pltpu.roll(first, LANES - shift, 1)
            high = sign * pltpu.roll(last, shift, 1)
            if shift == 2:
                low = jnp.where(even, low, pltpu.roll(last, 1, 1))
                high = jnp.where(even, pltpu.roll(first, LANES - 1, 1), high)
            buf[t, comp, :, strip(-1)] = low
            buf[t, comp, :, strip(strips)] = high


def stage(dst, src, base, weight, length, field, tiles, shift, cell, strips, group):
    factor = length / (2.0 * cell)
    drag = FRICTION * length
    sub, lane = iotas()
    rows_high = sub >= ROWS - shift
    rows_low = sub < shift
    lanes_high = lane >= LANES - shift
    lanes_low = lane < shift
    slots = dst.shape[0]
    group = min(group, strips)

    def block(g, carry):
        for j in range(group):
            k = g * group + j
            here = strip(k)
            cache = {}

            def get(comp, t):
                t = min(max(t, 0), slots - 1)
                if (comp, t) not in cache:
                    cache[comp, t] = src[t, comp, :, here]
                return cache[comp, t]

            for t in tiles:
                height, east, north = get(0, t), get(1, t), get(2, t)

                def row_diff(comp, centre):
                    before = jnp.where(rows_high, get(comp, t - 1), centre)
                    after = jnp.where(rows_low, get(comp, t + 1), centre)
                    return pltpu.roll(after, ROWS - shift, 0) - pltpu.roll(before, shift, 0)

                def col_diff(comp, centre):
                    before = jnp.where(lanes_high, src[t, comp, :, strip(k - 1)], centre)
                    after = jnp.where(lanes_low, src[t, comp, :, strip(k + 1)], centre)
                    return pltpu.roll(after, LANES - shift, 1) - pltpu.roll(before, shift, 1)

                b = field[t, :, pl.ds(here.start - LANES, LANES)]
                dx, dy = row_diff(0, height), col_diff(0, height)
                rise = row_diff(1, east) + col_diff(2, north)
                if base is src:
                    new_height = weight * height - factor * rise
                    new_east = (weight - drag) * east + factor * (b * dy - dx)
                    new_north = (weight - drag) * north - factor * (b * dx + dy)
                else:
                    old = [base[t, comp, :, here] for comp in range(3)]
                    if weight != 1.0:
                        old = [weight * o for o in old]
                    new_height = old[0] - factor * rise
                    new_east = old[1] - drag * east + factor * (b * dy - dx)
                    new_north = old[2] - drag * north - factor * (b * dx + dy)
                dst[t, 0, :, here] = new_height
                dst[t, 1, :, here] = new_east
                dst[t, 2, :, here] = new_north
        return carry

    lax.fori_loop(0, strips // group, block, 0)
    guards(dst, tiles, shift, strips)


def pair_mean(x, sub, lane):
    x = x + jnp.where(sub % 2 == 0, pltpu.roll(x, ROWS - 1, 0), pltpu.roll(x, 1, 0))
    x = x + jnp.where(lane % 2 == 0, pltpu.roll(x, LANES - 1, 1), pltpu.roll(x, 1, 1))
    return 0.25 * x


def flip_tiles(position, count, halo, first, copy_row):
    low = jnp.maximum(halo - position, 0)
    high = jnp.maximum(position + halo - (count - 1), 0)

    def fill_low(q, carry):
        for r in range(ROWS):
            copy_row(first + halo - position - 1 - q, ROWS - 1 - r, first + halo - position + q, r)
        return carry

    def fill_high(q, carry):
        for r in range(ROWS):
            copy_row(
                first + count + q - position + halo,
                ROWS - 1 - r,
                first + count - 1 - q - position + halo,
                r,
            )
        return carry

    lax.fori_loop(0, low, fill_low, 0)
    lax.fori_loop(0, high, fill_high, 0)


def flip_state(buf, position, count, halo, first=0):
    cols = pl.ds(LANES, buf.shape[3] - 2 * LANES)

    def copy_row(t_to, r_to, t_from, r_from):
        for comp, sign in ((0, 1.0), (1, -1.0), (2, 1.0)):
            buf[t_to, comp, pl.ds(r_to, 1), cols] = sign * buf[t_from, comp, pl.ds(r_from, 1), cols]

    flip_tiles(position, count, halo, first, copy_row)


def flip_field(field, position, count, halo):
    def copy_row(t_to, r_to, t_from, r_from):
        field[t_to, pl.ds(r_to, 1), :] = -field[t_from, pl.ds(r_from, 1), :]

    flip_tiles(position, count, halo, 0, copy_row)


def folded(left, right, lane):
    return jnp.where(lane % 2 == 0, left, right)


def unfolded(x, lane):
    left = jnp.where(lane % 2 == 0, x, pltpu.roll(x, 1, 1))
    right = jnp.where(lane % 2 == 1, x, pltpu.roll(x, LANES - 1, 1))
    return left, right


def zipped(even, odd, sub):
    return jnp.where(sub % 2 == 0, even, odd)


def unzipped(x, sub):
    even = jnp.where(sub % 2 == 0, x, pltpu.roll(x, 1, 0))
    odd = jnp.where(sub % 2 == 1, x, pltpu.roll(x, ROWS - 1, 0))
    return even, odd


def places(position):
    core = lax.rem(position, 2)
    chip = lax.div(position, 2)
    side = 1 - 2 * core
    near = 2 * (2 * lax.rem(chip, 2) - 1)
    far = 4 * (2 * lax.rem(lax.div(chip, 2), 2) - 1)
    return side, near, far


def fine_kernel(
    count, strips, pos, state, field, near_a, near_b, third, sib, sib_a, sib_b, coarse,
    out, detail, message, one, two, window,
):
    position = pos[0]
    side, near, _ = places(position)
    cols = pl.ds(LANES, strips * LANES)
    arrived = (
        (near_a, near), (near_b, -near), (third, -3 * side),
        (sib, side), (sib_a, near + side), (sib_b, side - near),
    )
    window[3] = LORENTZ * field[...]
    for comp in range(3):
        one[3, comp, :, cols] = state[comp]
    for ref, offset in arrived:
        slot = 3 + offset
        window[slot] = LORENTZ * ref[3]
        for comp in range(3):
            one[slot, comp, :, cols] = ref[comp]
    flip_field(window, position, count, 3)
    flip_state(one, position, count, 3)
    guards(one, range(7), 1, strips)

    run = functools.partial(stage, field=window, shift=1, cell=1.0, strips=strips, group=GROUP)
    a, b = one, two
    for reach, quads, lines in ((3, 3, 2), (2, 3, 2), (1, 2, 4)):
        tiles = range(3 - reach, 4 + reach)

        def quad(step, carry, a=a, b=b, tiles=tiles):
            run(b, a, a, QUAD_A, QUAD_B * TIME_STEP, tiles=tiles)
            run(a, b, a, 1.0, TIME_STEP, tiles=tiles)
            return carry

        lax.fori_loop(0, quads, quad, 0)
        for n in range(lines):
            if n == lines - 1:
                tiles = range(4 - reach, 3 + reach)
            run(b, a, a, 1.0, ALPHA * TIME_STEP, tiles=tiles)
            a, b = b, a

    sub, lane = iotas()
    keep = jnp.where(pos[1] == 0, 0.0, 1.0)
    half = strips // 2
    for k in range(half):
        means = []
        for comp in range(3):
            sides = []
            both = unfolded(coarse[comp, :, pl.ds(k * LANES, LANES)], lane)
            for s, less in zip((k, k + half), both):
                lanes = pl.ds(s * LANES, LANES)
                value = a[3, comp, :, strip(s)]
                out[comp, :, lanes] = value
                rest = value - keep * less
                detail[comp, :, lanes] = rest
                sides.append(pair_mean(rest, sub, lane))
            means.append(folded(*sides, lane))
        sides = [pair_mean(field[:, pl.ds(s * LANES, LANES)], sub, lane) for s in (k, k + half)]
        lanes = pl.ds(k * LANES, LANES)
        message[0, :, lanes] = zipped(means[0], means[1], sub)
        message[1, :, lanes] = zipped(means[2], LORENTZ * folded(*sides, lane), sub)


def coarse_step(bufs, field, tiles_of, strips, group):
    one, two, three = bufs
    length = FINE_STEPS * TIME_STEP
    run = functools.partial(stage, base=one, field=field, shift=2, cell=2.0, strips=strips, group=group)
    run(two, one, weight=1.0, length=length / 3.0, tiles=tiles_of(0))
    run(three, two, weight=1.0, length=length / 2.0, tiles=tiles_of(1))
    run(one, three, weight=1.0, length=length, tiles=tiles_of(2))


def coarse_kernel(
    count, strips, pos, state, field, sib, sib_a, sib_b, out, short, one, two, three, window
):
    position = pos[0]
    side, near, _ = places(position)
    sub, lane = iotas()
    half = strips // 2

    def put(slot, ref, plane):
        for k in range(half):
            pairs = [pl.ds(s * LANES, LANES) for s in (k, k + half)]
            for comp in range(3):
                means = [pair_mean(ref[comp, :, lanes], sub, lane) for lanes in pairs]
                one[slot, comp, :, strip(k)] = folded(*means, lane)
            means = [pair_mean(plane[:, lanes], sub, lane) for lanes in pairs]
            window[slot, :, pl.ds(k * LANES, LANES)] = LORENTZ * folded(*means, lane)

    put(1, state, field)
    put(1 + side, sib, sib.at[3])
    for ref, sign in ((sib_a, 1), (sib_b, -1)):

        @pl.when(sign * near + side == -side)
        def _(ref=ref):
            put(1 - side, ref, ref.at[3])

    flip_field(window, position, count, 1)
    flip_state(one, position, count, 1)
    guards(one, range(3), 2, half)
    coarse_step((one, two, three), window, lambda n: range(3) if n < 2 else (1,), half, GROUP)
    for k in range(half):
        for comp in range(3):
            value = one[1, comp, :, strip(k)]
            short[comp, :, pl.ds(k * LANES, LANES)] = value
            for s, part in zip((k, k + half), unfolded(value, lane)):
                out[comp, :, pl.ds(s * LANES, LANES)] = part


def powers_kernel(
    count, strips, pos, own, sib, near_a, near_b, far_a, far_b, fifth, others, *refs
):
    outs, (one, two, three, window) = refs[:3], refs[3:]
    position = pos[0]
    side, near, far = places(position)
    sub, lane = iotas()
    half = strips // 2
    arrived = (
        (own, 0, 0), (sib, 0, side), (near_a, 0, near), (near_b, 0, -near), (far_a, 0, far),
        (far_b, 0, -far), (fifth, 0, -5 * side), (others, 0, near + side),
        (others, 2, side - near), (others, 4, far + side), (others, 6, side - far),
    )
    for ref, at, offset in arrived:
        slot = 5 + offset
        for k in range(half):
            lanes = pl.ds(k * LANES, LANES)
            height, east = unzipped(ref[at, :, lanes], sub)
            north, plane = unzipped(ref[at + 1, :, lanes], sub)
            one[slot, 0, :, strip(k)] = height
            one[slot, 1, :, strip(k)] = east
            one[slot, 2, :, strip(k)] = north
            window[slot, :, lanes] = plane
    flip_field(window, position, count, 5)
    flip_state(one, position, count, 5)
    guards(one, range(11), 2, half)
    for s in range(6):

        def tiles_of(n, s=s):
            reach = -(-2 * (18 - 3 * s - n - 1) // ROWS)
            return range(5 - reach, 6 + reach)

        coarse_step((one, two, three), window, tiles_of, half, 8)
        out = outs[s // 2]
        for k in range(half):
            lanes = pl.ds(k * LANES, LANES)
            height, east, north = [one[5, comp, :, strip(k)] for comp in range(3)]
            out[s % 2, :, lanes] = zipped(height, east, sub)
            if s % 2 == 0:
                out[2, :, lanes] = north
            else:
                out[2, :, lanes] = zipped(out[2, :, lanes], north, sub)


def final_kernel(strips, pos, own, other, detail, anchor, out):
    sub, lane = iotas()
    half = strips // 2
    first = pos[1] == 0
    for k in range(half):
        lanes = pl.ds(k * LANES, LANES)
        height, east = unzipped(own[0, :, lanes] + other[0, :, lanes], sub)
        north = unzipped(own[2, :, lanes], sub)[0] + unzipped(other[1, :, lanes], sub)[1]
        for comp, value in enumerate((height, east, north)):
            for s, part in zip((k, k + half), unfolded(value, lane)):
                wide = pl.ds(s * LANES, LANES)
                total = part + detail[comp, :, wide]
                out[comp, :, wide] = jnp.where(first, anchor[comp, :, wide], total)


def call(kernel, outs, buffers, name, *args):
    return pl.pallas_call(
        kernel,
        out_shape=outs,
        in_specs=[SMEM] + [VMEM] * (len(args) - 1),
        out_specs=[VMEM] * len(outs),
        scratch_shapes=buffers,
        compiler_params=pltpu.CompilerParams(vmem_limit_bytes=48 * 1024 * 1024),
        name=name,
    )(*args)


def swap(block, partner):
    slices, count = lax.axis_size("tm"), lax.axis_size("space")
    pairs = [(i, partner(i)) for i in range(count)]
    pairs = [(i, j) for i, j in pairs if 0 <= j < count]
    return lax.ppermute(block, "space", pairs)


def later(block, distance):
    slices = lax.axis_size("tm")
    return lax.ppermute(block, "tm", [(m, m + distance) for m in range(slices - distance)])


def two_legs():
    slices, count = lax.axis_size("tm"), lax.axis_size("space")
    run = min(8, count // 2)
    legs = [], []
    for m in range(slices - 1):
        for i in range(count):
            y, upper = divmod(m, 2)
            group, low = divmod(i // 2, run)
            way = 1 if i % 2 == 0 else -1
            upper, low = divmod((upper * run + low + way * (run // 2)) % (2 * run), run)
            stop = (2 * y + upper) * count + 2 * (group * run + low) + i % 2
            legs[0].append((m * count + i, stop))
            legs[1].append((stop, (m + 1) * count + i))
    return legs


def sibling(i):
    return i + 1 - 2 * (i % 2)


def near_odd(i):
    return i + (2 if (i // 2) % 2 == 1 else -2)


def near_even(i):
    return i - (2 if (i // 2) % 2 == 1 else -2)


def far_odd(i):
    return i + (4 if (i // 4) % 2 == 1 else -4)


def far_even(i):
    return i - (4 if (i // 4) % 2 == 1 else -4)


def third(i):
    return i - 3 if i % 2 == 0 else i + 3


def fifth(i):
    return i - 5 if i % 2 == 0 else i + 5


def body(start_state, vertical_field):
    state = start_state[0]
    cols = state.shape[2]
    strips = cols // LANES
    count = lax.axis_size("space")
    pos = jnp.stack([lax.axis_index("space"), lax.axis_index("tm")]).astype(jnp.int32)
    shape = lambda *dims: jax.ShapeDtypeStruct(dims, jnp.float32)
    tile = shape(3, ROWS, cols)
    buf = lambda tiles, wide: pltpu.VMEM((tiles, 3, ROWS, wide + 2 * LANES), jnp.float32)
    plane = lambda tiles, wide: pltpu.VMEM((tiles, ROWS, wide), jnp.float32)

    sent = jnp.concatenate([state, vertical_field[None]], axis=0)
    sib = swap(sent, sibling)
    b = swap(sent, near_even)
    q = swap(sent, third)
    a = swap(sent, near_odd)
    a, b, q = lax.optimization_barrier((a, b, q))
    sib_b, sib_a = swap(b, sibling), swap(a, sibling)
    coarse_end, short = call(
        functools.partial(coarse_kernel, count, strips),
        [tile, shape(3, ROWS, cols // 2)],
        [buf(3, cols // 2)] * 3 + [plane(3, cols // 2)],
        "coarse",
        pos, state, vertical_field, sib, sib_a, sib_b,
    )
    fine_end, detail, message = call(
        functools.partial(fine_kernel, count, strips),
        [tile, tile, shape(2, ROWS, cols // 2)],
        [buf(7, cols), buf(7, cols), plane(7, cols)],
        "fine",
        pos, state, vertical_field, a, b, q, sib, sib_a, sib_b, short,
    )
    legs = two_legs()
    halfway = lax.ppermute(detail, ("tm", "space"), legs[0])
    sib = swap(message, sibling)
    b = swap(message, near_even)
    d = swap(message, far_even)
    q = swap(message, fifth)
    c = swap(message, far_odd)
    a = swap(message, near_odd)
    a, b, c, d, q, sib = lax.optimization_barrier((a, b, c, d, q, sib))
    others = swap(jnp.concatenate([a, b, c, d], axis=0), sibling)
    powers = call(
        functools.partial(powers_kernel, count, strips),
        [shape(3, ROWS, cols // 2)] * 3,
        [buf(11, cols // 2)] * 3 + [plane(11, cols // 2)],
        "powers",
        pos, message, sib, a, b, c, d, q, others,
    )
    own = sum(later(x, 2 * d + 2) for d, x in enumerate(powers))
    arrived = lax.ppermute(halfway, ("tm", "space"), legs[1])
    other = later(own[1:], 1)
    (new_start,) = call(
        functools.partial(final_kernel, strips),
        [tile],
        [],
        "final",
        pos, own, other, arrived, state,
    )
    return (new_start[None], fine_end[None], coarse_end[None])


def solution(mesh):
    in_specs = (P("tm", None, "space", None), P("space", None))
    out_specs = (
        P("tm", None, "space", None),
        P("tm", None, "space", None),
        P("tm", None, "space", None),
    )
    return jax.shard_map(body, mesh=mesh, in_specs=in_specs, out_specs=out_specs, check_vma=False)
```
